32 devices in a mesh: groups: 2 (over y), frame: 4 (over z), tok: 2 (over x), head: 2 (over core).
Axes of the slice: x: 2, y: 2, z: 4, core: 2. Of those that a mesh axis runs over, the one named last changes fastest.
Arguments:
- frames: bfloat16 [8, 1024, 1152], P(('groups', 'frame'), 'tok'), parts along dimension 0, may hold values from -6 to 6
- modulation: float32 [3, 1152], replicated, may hold values from -4.1 to 6, as said below
- w_qkv: bfloat16 [1152, 16, 3, 72], P('frame', 'head'), may hold values from -0.1875 to 0.1875
- w_out: bfloat16 [1152, 1152], P('head', 'frame'), may hold values from -0.1875 to 0.1875
- anchor_offsets: int32 [2], P('groups'), parts along dimension 0, may hold values from 0 to 3
Outputs:
- updated: bfloat16 [8, 1024, 1152], P(('groups', 'frame'), 'tok', 'head'), parts along dimension 0
The draws below stay inside these ranges and needn't reach their ends.
There are 2 independent parts, one for each index of `groups`. The reference program is written for one: setup_inputs(seed, part) draws one part's arguments, and reference() takes and returns one part's arrays. A program takes and returns all parts, laid end to end along the dimension named above; an argument that names none is the same for every part. Nothing has to cross between parts.
Inputs may be any that keep to these rules, and one draw needn't show every extreme that they name: anchor_offsets[c] is the offset, within span c of 4 frames, of the frame that all frames of the span attend to. `modulation`: row 0 is the shift, row 1 the scale, row 2 the gate.
All inputs are finite; a program needn't handle non-finite values.
Results may differ from the reference program's by a relative error of at most 0.0049.
The reference program's roundings to bfloat16 on the way count: a program that leaves them out, or rounds other values in their place, can miss the bound.
Values may be sent and summed in bfloat16 or wider, within the bound.
No kernel may reach another device: no remote copies, remote signals or barrier semaphores. Data moves between devices by JAX's collectives and lax.ppermute only.
A program may use at most 64 MiB of HBM per device.

```python
import jax
import jax.numpy as jnp
from jax import lax

D = 1152
HEADS = 16
HD = 72
FTOK = 1024
FRAMES = 4
SPAN = 4
SPANS = 1


def draw_modulation(key, part):
    key_shift, key_scale, key_sign, key_gate = jax.random.split(jax.random.fold_in(key, 11), 4)
    shift_vec = jnp.clip(0.5 * jax.random.normal(key_shift, (D,), jnp.float32), -2.0, 2.0)
    scale_vec = jax.random.uniform(key_scale, (D,), jnp.float32, -0.5, 1.0)
    sign_vec = jnp.where(jax.random.bernoulli(key_sign, 0.5, (D,)), 1.0, -1.0)
    gate_vec = sign_vec * jnp.exp(jax.random.uniform(key_gate, (D,), jnp.float32, 0.0, 1.4))
    return jnp.stack([shift_vec, scale_vec, gate_vec]).astype(jnp.float32)


def block_scale(stream_key, dims, cuts, low, high):
    def one(position, shards_of):
        steps = jax.random.uniform(jax.random.fold_in(jax.random.fold_in(stream_key, 6), position), (shards_of,), jnp.float32, low / len(cuts), high / len(cuts))
        return jnp.repeat(jnp.exp(steps), dims[position] // shards_of).reshape((-1,) + (1,) * (len(dims) - position - 1))

    loudness = one(*cuts[0])
    for cut in cuts[1:]:
        loudness = loudness * one(*cut)
    return loudness


def bell_draw(own_key, extent, spread, most, cuts=(), held_as=jnp.bfloat16):
    level = block_scale(own_key, extent, cuts, -0.22, 0.18) if cuts else 1.0
    entries = jax.random.normal(own_key, extent, jnp.float32) * spread * level
    return jnp.minimum(jnp.maximum(entries, -most), most).astype(held_as)


def setup_inputs(seed: int = 0, part: int = 0) -> dict:
    keys = jax.random.split(jax.random.key(seed), 6)
    part_keys = jax.random.split(jax.random.fold_in(keys[5], part), 6)
    return {
        "frames": bell_draw(part_keys[0], (FRAMES, FTOK, D), 1.0, 6.0, ((0, 4), (1, 2))),
        "modulation": draw_modulation(jax.random.fold_in(keys[5], 71), part),
        "w_qkv": bell_draw(keys[2], (D, HEADS, 3, HD), D ** -0.5, 0.1875, ((0, 4), (1, 2))),
        "w_out": bell_draw(keys[3], (HEADS * HD, D), (HEADS * HD) ** -0.5, 0.1875, ((0, 2), (1, 4))),
        "anchor_offsets": jax.random.randint(part_keys[4], (SPANS,), 0, SPAN).astype(jnp.int32),
    }


def normalize(frame_data, modulation):
    values = frame_data.astype(jnp.float32)
    row_mean = lax.optimization_barrier(jnp.mean(values, axis=-1, keepdims=True))
    centred = values - row_mean
    row_var = lax.optimization_barrier(jnp.mean(centred * centred, axis=-1, keepdims=True))
    normed = centred * lax.rsqrt(row_var + 1e-06)
    return (normed * (1.0 + modulation[1]) + modulation[0]).astype(jnp.bfloat16)

def reference(frames, modulation, w_qkv, w_out, anchor_offsets):
    flat_weight = w_qkv.reshape(D, HEADS * 3 * HD)

    def project(frame_data):
        mixed = jnp.dot(normalize(frame_data, modulation), flat_weight, preferred_element_type=jnp.float32)
        return mixed.astype(jnp.bfloat16).reshape(FTOK, HEADS, 3, HD)

    def key_values(frame_data):
        mixed = project(frame_data)
        return (mixed[:, :, 1, :], mixed[:, :, 2, :])
    all_keys, all_vals = lax.map(key_values, frames)

    def one_frame(frame_idx):
        frame_data = frames[frame_idx]
        query = project(frame_data)[:, :, 0, :]
        span_idx = frame_idx // SPAN
        anchor = span_idx * SPAN + anchor_offsets[span_idx]
        prev_idx = jnp.maximum(frame_idx - 1, 0)
        key_rows = jnp.concatenate([all_keys[anchor], all_keys[prev_idx], all_keys[frame_idx]], 0)
        val_rows = jnp.concatenate([all_vals[anchor], all_vals[prev_idx], all_vals[frame_idx]], 0)
        use_prev = frame_idx > 0
        use_anchor = (anchor != frame_idx) & (anchor != frame_idx - 1)
        valid_keys = jnp.concatenate([jnp.broadcast_to(use_anchor, (FTOK,)), jnp.broadcast_to(use_prev, (FTOK,)), jnp.ones((FTOK,), bool)])
        scores = jnp.einsum('qhd,khd->hqk', query.astype(jnp.float32), key_rows.astype(jnp.float32)) * HD ** (-0.5)
        scores = jnp.where(valid_keys[None, None, :], scores, -1e+30)
        row_max = lax.optimization_barrier(jnp.max(scores, axis=-1, keepdims=True))
        probs = jnp.exp(scores - row_max)
        denominator = lax.optimization_barrier(jnp.sum(probs, axis=-1, keepdims=True))
        probs_b = probs.astype(jnp.bfloat16)
        numerator = jnp.einsum('hqk,khd->hqd', probs_b.astype(jnp.float32), val_rows.astype(jnp.float32))
        attended = (numerator / denominator).astype(jnp.bfloat16)
        attended = jnp.transpose(attended, (1, 0, 2)).reshape(FTOK, HEADS * HD)
        projected = jnp.dot(attended, w_out, preferred_element_type=jnp.float32)
        return (frame_data.astype(jnp.float32) + modulation[2] * projected).astype(jnp.bfloat16)
    return lax.map(one_frame, jnp.arange(FRAMES, dtype=jnp.int32))
```

```python
import functools
import math

import jax
import jax.numpy as jnp
from jax import lax
from jax.experimental import pallas as pl
from jax.experimental.pallas import tpu as pltpu
from jax.sharding import PartitionSpec as P

VMEM_LIMIT = 56 * 2**20


def dot_nn(a, b):
    return lax.dot_general(a, b, (((1,), (0,)), ((), ())), preferred_element_type=jnp.float32)


def dot_nt(a, b):
    return lax.dot_general(a, b, (((1,), (1,)), ((), ())), preferred_element_type=jnp.float32)


def call(kernel, out_shape, operands, scratch=(), flops=0, moved=0):
    smem = pl.BlockSpec(memory_space=pltpu.SMEM)
    vmem = pl.BlockSpec(memory_space=pltpu.VMEM)
    many = isinstance(out_shape, (list, tuple))
    return pl.pallas_call(
        kernel,
        out_shape=out_shape,
        in_specs=[smem if x.dtype == jnp.int32 else vmem for x in operands],
        out_specs=[vmem] * len(out_shape) if many else vmem,
        scratch_shapes=list(scratch),
        compiler_params=pltpu.CompilerParams(vmem_limit_bytes=VMEM_LIMIT),
        cost_estimate=pl.CostEstimate(flops=flops, bytes_accessed=moved, transcendentals=0),
    )(*operands)


def project_kernel(kv_width, place_ref, mine_ref, other_ref, mod_ref, weight_ref, kv_ref, q_ref, hidden):
    half = mine_ref.shape[0]
    for part, ref in ((place_ref[0], mine_ref), (1 - place_ref[0], other_ref)):
        values = ref[...].astype(jnp.float32)
        row_mean = jnp.mean(values, axis=-1, keepdims=True)
        centred = values - row_mean
        row_var = jnp.mean(centred * centred, axis=-1, keepdims=True)
        normed = centred * lax.rsqrt(row_var + 1e-06)
        normed = normed * (1.0 + mod_ref[1:2, :]) + mod_ref[0:1, :]
        hidden[pl.ds(pl.multiple_of(part * half, half), half), :] = normed.astype(jnp.bfloat16)
    mixed = dot_nt(weight_ref[...], hidden[...]).astype(jnp.bfloat16)
    kv_ref[...] = mixed[:kv_width]
    q_ref[...] = mixed[kv_width:]


def project(place, mine, other, modulation, weight, kv_width):
    half, width = mine.shape
    rows = 2 * half
    out_width = weight.shape[0]
    return call(
        functools.partial(project_kernel, kv_width),
        (
            jax.ShapeDtypeStruct((kv_width, rows), jnp.bfloat16),
            jax.ShapeDtypeStruct((out_width - kv_width, rows), jnp.bfloat16),
        ),
        (place, mine, other, modulation, weight),
        [pltpu.VMEM((rows, width), jnp.bfloat16)],
        flops=2 * rows * width * out_width,
        moved=2 * (rows * width + width * out_width + rows * out_width),
    )


def attend_kernel(count, heads, head_dim, *refs):
    ids_ref = refs[0]
    q_refs = refs[1 : 1 + count]
    near_refs = refs[1 + count : 1 + 2 * count]
    far_refs = refs[1 + 2 * count : 1 + 3 * count]
    out_ref = refs[1 + 3 * count]
    (q_all, k_all, v_all, even_scores, odd_scores, high, block_high, scale_old, total, q_list, k_list) = refs[2 + 3 * count :]
    rows = q_refs[0].shape[1]
    factor = math.log2(math.e) / math.sqrt(head_dim)
    value_rows = v_all.shape[1]
    ones = jnp.ones((value_rows - head_dim, rows), jnp.float32)
    for slot in range(count):
        frame = ids_ref[slot]
        queries = q_refs[slot][...].astype(jnp.float32)
        for head in range(heads):
            q_all[frame * heads + head] = queries[head * head_dim : (head + 1) * head_dim].astype(jnp.bfloat16)
        for side, ref in ((0, near_refs[slot]), (1, far_refs[slot])):
            keyvals = ref[...].astype(jnp.float32)
            span = pl.ds(side * rows, rows)
            for head in range(heads):
                keys = keyvals[head * head_dim : (head + 1) * head_dim]
                k_all[frame * heads + head, span, :] = keys.T.astype(jnp.bfloat16)
                first = (heads + head) * head_dim
                values = jnp.concatenate([keyvals[first : first + head_dim], ones], 0)
                v_all[frame * heads + head, :, span] = values.astype(jnp.bfloat16)
    anchor = ids_ref[count]
    items = jnp.int32(0)
    for frame in range(count):
        q_list[items] = frame
        k_list[items] = frame
        items += 1
        if frame > 0:
            q_list[items] = frame
            k_list[items] = frame - 1
            items += 1
        q_list[items] = frame
        k_list[items] = anchor
        items += jnp.where((anchor != frame) & (anchor != frame - 1), 1, 0)
    high[...] = jnp.full_like(high, -1e30)
    total[...] = jnp.zeros_like(total)
    scores_of = (even_scores, odd_scores)
    spare = count * heads
    key_rows = 2 * rows
    step = math.gcd(key_rows, 256)

    def stage(head_a, item_a, live_a, head_b, item_b, live_b):
        slot_a = q_list[item_a] * heads + head_a
        state_a = jnp.where(live_a, slot_a, spare)
        key_a = k_list[item_a] * heads + head_a
        state_b = jnp.where(live_b, q_list[item_b] * heads + head_b, spare)
        key_b = k_list[item_b] * heads + head_b
        queries = q_all[slot_a]
        top_b = block_high[head_b]
        running = total[state_b] * scale_old[head_b]
        old = high[state_a]
        top = old
        for start in range(0, key_rows, step):
            part = pl.ds(start, step)
            scores = dot_nn(k_all[key_a, part, :], queries)
            scores_of[head_a][part, :] = scores
            top = jnp.maximum(top, jnp.max(scores, axis=0, keepdims=True))
            probs = jnp.exp2((scores_of[head_b][part, :] - top_b) * factor).astype(jnp.bfloat16)
            running = running + dot_nn(v_all[key_b, :, part], probs)
        total[state_b] = running
        scale_old[head_a] = jnp.exp2((old - top) * factor)
        block_high[head_a] = top
        high[state_a] = top

    def body(index, carry):
        now = jnp.minimum(index, items - 1)
        before = jnp.maximum(index - 1, 0)
        stage(0, now, index < items, 1, before, index > 0)
        stage(1, now, index < items, 0, now, index < items)
        return carry

    lax.fori_loop(0, items + 1, body, 0)
    for frame in range(count):
        parts = []
        for head in range(heads):
            sums = total[frame * heads + head]
            parts.append(sums[:head_dim] / sums[head_dim : head_dim + 1])
        out_ref[frame] = jnp.concatenate(parts, 0).astype(jnp.bfloat16)


def attend_all(ids, queries, near, far, heads, head_dim):
    count = len(queries)
    rows = queries[0].shape[1]
    value_rows = head_dim + 8
    states = count * heads + 1
    return call(
        functools.partial(attend_kernel, count, heads, head_dim),
        jax.ShapeDtypeStruct((count, heads * head_dim, rows), jnp.bfloat16),
        (ids, *queries, *near, *far),
        [
            pltpu.VMEM((count * heads, head_dim, rows), jnp.bfloat16),
            pltpu.VMEM((count * heads, 2 * rows, head_dim), jnp.bfloat16),
            pltpu.VMEM((count * heads, value_rows, 2 * rows), jnp.bfloat16),
            pltpu.VMEM((2 * rows, rows), jnp.float32),
            pltpu.VMEM((2 * rows, rows), jnp.float32),
            pltpu.VMEM((states, 1, rows), jnp.float32),
            pltpu.VMEM((heads, 1, rows), jnp.float32),
            pltpu.VMEM((heads, 1, rows), jnp.float32),
            pltpu.VMEM((states, value_rows, rows), jnp.float32),
            pltpu.SMEM((3 * count + 1,), jnp.int32),
            pltpu.SMEM((3 * count + 1,), jnp.int32),
        ],
        flops=3 * count * heads * rows * 2 * rows * head_dim * 4,
        moved=2 * count * heads * head_dim * rows * 6,
    )


def finish_kernel(near_w, far_w, near_ref, far_ref, frame_ref, gate_ref, out_ref):
    projected = dot_nn(near_w[...], near_ref[...]) + dot_nn(far_w[...], far_ref[...])
    updated = frame_ref[...].astype(jnp.float32) + gate_ref[...] * projected
    out_ref[...] = updated.astype(jnp.bfloat16)


def finish(near_w, far_w, near, far, frame_part, gate_part):
    return call(
        finish_kernel,
        jax.ShapeDtypeStruct(frame_part.shape, jnp.bfloat16),
        (near_w, far_w, near, far, frame_part, gate_part),
        flops=4 * near_w.shape[0] * near_w.shape[1] * near.shape[1],
        moved=4 * (near_w.size + near.size + frame_part.size),
    )


def swapped(block, axis):
    return lax.ppermute(block, axis, [(0, 1), (1, 0)])


def shifted(block, axis, distance):
    devices = range(lax.axis_size(axis))
    route = [(i - distance, i) for i in devices if i - distance in devices]
    return lax.ppermute(block, axis, route)


def from_partner(block, axis, stride):
    count = lax.axis_size(axis)
    route = []
    for low in range(count):
        high = low | 1 << stride
        if high != low and high < count:
            route += [(low, high), (high, low)]
    return lax.ppermute(block, axis, route)


def attend(queries, kv_all, first_frame, anchor, head_dim):
    frame_count, query_rows, query_width = queries.shape
    key_count = kv_all.shape[1]
    head_count = query_width // head_dim
    block_rows = math.gcd(512, query_rows)
    kv_heads = kv_all.reshape(frame_count + 2, key_count, head_count, 2, head_dim)
    global_idx = first_frame + 0
    use_prev = global_idx > 0
    use_anchor = (anchor != global_idx) & (anchor != global_idx - 1)
    valid_keys = jnp.concatenate(
        [
            jnp.broadcast_to(use_anchor, (key_count,)),
            jnp.broadcast_to(use_prev, (key_count,)),
            jnp.ones((key_count,), bool),
        ]
    )
    frame_queries = queries[0]

    def one_head(head_idx):
        picked = lax.dynamic_index_in_dim(kv_heads, head_idx, 2, keepdims=False)
        key_rows = jnp.concatenate(
            [picked[frame_count + 1, :, 0], picked[frame_count, :, 0], picked[0, :, 0]], 0
        )
        val_rows = jnp.concatenate(
            [picked[frame_count + 1, :, 1], picked[frame_count, :, 1], picked[0, :, 1]], 0
        )
        query_head = lax.dynamic_slice_in_dim(frame_queries, head_idx * head_dim, head_dim, 1)
        query_blocks = query_head.reshape(query_rows // block_rows, block_rows, head_dim)

        def one_block(query_block):
            scores = lax.dot_general(
                query_block, key_rows, (((1,), (1,)), ((), ())), preferred_element_type=jnp.float32
            ) * head_dim ** (-0.5)
            scores = jnp.where(valid_keys[None, :], scores, -1e30)
            row_max = jnp.max(scores, axis=-1, keepdims=True)
            probs = jnp.exp(scores - row_max)
            denominator = jnp.sum(probs, axis=-1, keepdims=True)
            numerator = jnp.dot(
                probs.astype(jnp.bfloat16), val_rows, preferred_element_type=jnp.float32
            )
            return (numerator / denominator).astype(jnp.bfloat16)

        return lax.map(one_block, query_blocks).reshape(query_rows, head_dim)

    per_head = lax.map(one_head, jnp.arange(head_count, dtype=jnp.int32))
    frame_outputs = [jnp.transpose(per_head, (1, 0, 2)).reshape(query_rows, head_count * head_dim)]
    return jnp.stack(frame_outputs)


def by_frames(frames, modulation, w_qkv, w_out, anchor_offsets):
    frame_count, row_count, model_width = frames.shape
    head_local = w_qkv.shape[1]
    head_dim = w_qkv.shape[3]
    my_index = lax.axis_index("frame")
    flat_rows = frames.reshape(frame_count * row_count, model_width).astype(jnp.float32)
    row_mean = jnp.mean(flat_rows, axis=-1, keepdims=True)
    centred = flat_rows - row_mean
    row_var = jnp.mean(centred * centred, axis=-1, keepdims=True)
    normed = centred * lax.rsqrt(row_var + 1e-06)
    hidden = (normed * (1.0 + modulation[1]) + modulation[0]).astype(jnp.bfloat16)
    full_weight = lax.all_gather(w_qkv, "frame", axis=0, tiled=True)
    mixed = jnp.dot(
        hidden,
        full_weight.reshape(model_width, head_local * 3 * head_dim),
        preferred_element_type=jnp.float32,
    )
    mixed = mixed.astype(jnp.bfloat16).reshape(frame_count, row_count, head_local, 3, head_dim)
    queries = mixed[:, :, :, 0, :].reshape(frame_count, row_count, head_local * head_dim)
    keyvals = mixed[:, :, :, 1:, :].reshape(frame_count, row_count, head_local * 2 * head_dim)
    span_count = anchor_offsets.shape[0]
    total_frames = frame_count * lax.axis_size("frame")
    span_len = total_frames // span_count
    first_frame = my_index * frame_count
    mine_span = first_frame // span_len
    anchor = mine_span * span_len + anchor_offsets[mine_span]
    prev_kv = shifted(keyvals[frame_count - 1], "frame", 1)
    holder = anchor // frame_count
    anchor_kv = lax.dynamic_index_in_dim(keyvals, anchor % frame_count, 0, keepdims=False)
    levels = (span_len // frame_count).bit_length() - 1
    for bit_index in range(levels):
        partner = from_partner(anchor_kv, "frame", bit_index)
        take_partner = my_index >> bit_index & 1 != holder >> bit_index & 1
        anchor_kv = jnp.where(take_partner, partner, anchor_kv)
    kv_all = jnp.concatenate([keyvals, prev_kv[None], anchor_kv[None]], 0)
    kv_whole = lax.all_gather(kv_all, "tok", axis=1, tiled=True)
    attended = attend(queries, kv_whole, first_frame, anchor, head_dim)
    flat_attended = attended.reshape(frame_count * row_count, head_local * head_dim)
    term_cols = jnp.dot(
        flat_attended,
        lax.all_gather(w_out, "frame", axis=1, tiled=True),
        preferred_element_type=jnp.float32,
    )
    summed = lax.psum_scatter(term_cols, "head", scatter_dimension=1, tiled=True)
    half_width = summed.shape[1]
    col_start = lax.axis_index("head") * half_width
    residual_in = lax.dynamic_slice_in_dim(flat_rows, col_start, half_width, 1)
    gate_part = lax.dynamic_slice_in_dim(modulation[2], col_start, half_width, 0)
    result = (residual_in + gate_part * summed).astype(jnp.bfloat16)
    return result.reshape(frame_count, row_count, half_width)


def line_gather(block, axis):
    count = lax.axis_size(axis)
    me = lax.axis_index(axis)
    middle = count // 2
    right, left, both = {}, {}, {}
    for d in range(1, middle):
        right[d] = lax.ppermute(block, axis, [(i, i + d) for i in range(count - d)])
        left[d] = lax.ppermute(block, axis, [(i + d, i) for i in range(count - d)])
    both[middle] = lax.ppermute(block, axis, [(i, i ^ middle) for i in range(count)])
    for d in range(middle + 1, count):
        route = [(i + d - 1, i + d) for i in range(count - d)] + [(i - d + 1, i - d) for i in range(d, count)]
        both[d] = lax.ppermute(both[d - 1], axis, route)
    found = []
    for d in range(1, middle):
        found.append((jnp.where(me >= d, me - d, me + d), jnp.where(me >= d, right[d], left[d])))
    found.append((me ^ middle, both[middle]))
    for d in range(1, middle):
        e = count - d
        inner = (me >= d) & (me < e)
        index = jnp.where(me < d, me + e, jnp.where(me >= e, me - e, me + d))
        found.append((index, jnp.where(inner, left[d], both[e])))
    return found


def by_heads(frames, modulation, w_qkv, w_out, anchor_offsets):
    _, rows, width = frames.shape
    share, head_local, _, head_dim = w_qkv.shape
    count = lax.axis_size("frame")
    heads = head_local // count
    core = lax.axis_index("head")
    me = lax.axis_index("frame")
    frame = frames[0]
    half = rows // 2
    mine = lax.dynamic_slice_in_dim(frame, core * half, half, 0)
    found = line_gather(mine, "frame")

    blocks = jnp.transpose(w_qkv, (1, 2, 3, 0)).reshape(count, heads, 3 * head_dim, share)
    group_count = lax.axis_size("groups")
    if group_count == 2 and heads == 2:
        group = lax.axis_index("groups")
        part = lax.dynamic_index_in_dim(blocks, group, 1, keepdims=False)
        part = lax.all_to_all(part, "frame", 0, 0)
        partner = swapped(part, "groups")
        per_head = [jnp.where(group == 0, part, partner), jnp.where(group == 0, partner, part)]
    else:
        whole = lax.all_to_all(blocks, "frame", 0, 0)
        per_head = [whole[:, h] for h in range(heads)]
    per_head = [jnp.transpose(w, (1, 0, 2)).reshape(3, head_dim, width) for w in per_head]
    weight = jnp.concatenate([w[kind] for kind in (1, 2, 0) for w in per_head], 0)
    kv_width = 2 * heads * head_dim

    queries, near, far, ids = [], [], [], []
    zero = jnp.zeros((1,), jnp.int32)
    place = core.reshape(1).astype(jnp.int32)
    for index, block in [(me, None)] + found:
        if block is None:
            kv, q = project(zero, frame[:half], frame[half:], modulation, weight, kv_width)
        else:
            kv, q = project(place, block, swapped(block, "head"), modulation, weight, kv_width)
        ids.append(index)
        queries.append(q)
        near.append(kv)
        far.append(swapped(kv, "tok"))
    ids = jnp.stack(ids + [anchor_offsets[0]]).astype(jnp.int32)
    attended = attend_all(ids, queries, near, far, heads, head_dim)
    arrived = lax.all_to_all(attended, "frame", 0, 0).reshape(count * heads * head_dim, rows)
    arrived_far = swapped(arrived, "head")

    out_half = width // 2
    w_cols = lax.all_gather(w_out.T, "frame", axis=0, tiled=True)
    near_w = lax.dynamic_slice_in_dim(w_cols, core * out_half, out_half, 0)
    far_w = swapped(lax.dynamic_slice_in_dim(w_cols, (1 - core) * out_half, out_half, 0), "head")
    frame_part = lax.dynamic_slice_in_dim(frame, core * out_half, out_half, 1).T
    gate_part = lax.dynamic_slice_in_dim(modulation[2], core * out_half, out_half, 0)[:, None]
    updated = finish(near_w, far_w, arrived, arrived_far, frame_part, gate_part)
    return updated.T[None]


def on_device(frames, modulation, w_qkv, w_out, anchor_offsets):
    count = lax.axis_size("frame")
    fits = (
        frames.shape[0] == 1
        and anchor_offsets.shape[0] == 1
        and count >= 2
        and count & (count - 1) == 0
        and lax.axis_size("head") == 2
        and lax.axis_size("tok") == 2
        and w_qkv.shape[1] % count == 0
        and w_qkv.shape[3] % 8 == 0
        and frames.shape[1] % 256 == 0
        and frames.shape[2] % 32 == 0
    )
    step = by_heads if fits else by_frames
    return step(frames, modulation, w_qkv, w_out, anchor_offsets)


def solution(mesh):
    placed = (
        P(("groups", "frame"), "tok", None),
        P(),
        P("frame", "head", None, None),
        P("head", "frame"),
        P("groups"),
    )
    return jax.shard_map(
        on_device,
        mesh=mesh,
        in_specs=placed,
        out_specs=P(("groups", "frame"), "tok", "head"),
        check_vma=False,
    )
```

```python
import functools
import math

import jax
import jax.numpy as jnp
from jax import lax
from jax.experimental import pallas as pl
from jax.experimental.pallas import tpu as pltpu
from jax.sharding import PartitionSpec as P

VMEM_LIMIT = 56 * 2**20


def dot_nn(a, b):
    return lax.dot_general(a, b, (((1,), (0,)), ((), ())), preferred_element_type=jnp.float32)


def dot_nt(a, b):
    return lax.dot_general(a, b, (((1,), (1,)), ((), ())), preferred_element_type=jnp.float32)


def call(kernel, out_shape, operands, scratch=(), flops=0, moved=0, left=()):
    smem = pl.BlockSpec(memory_space=pltpu.SMEM)
    vmem = pl.BlockSpec(memory_space=pltpu.VMEM)
    where = pl.BlockSpec(memory_space=pl.ANY)
    many = isinstance(out_shape, (list, tuple))
    return pl.pallas_call(
        kernel,
        out_shape=out_shape,
        in_specs=[where if i in left else smem if x.dtype == jnp.int32 else vmem for i, x in enumerate(operands)],
        out_specs=[vmem] * len(out_shape) if many else vmem,
        scratch_shapes=list(scratch),
        compiler_params=pltpu.CompilerParams(vmem_limit_bytes=VMEM_LIMIT),
        cost_estimate=pl.CostEstimate(flops=flops, bytes_accessed=moved, transcendentals=0),
    )(*operands)


def norm_kernel(place_ref, frame_ref, mod_ref, out_ref, rows, arrived):
    half = out_ref.shape[0]
    start = pl.multiple_of(place_ref[0] * half, half)
    copy = pltpu.make_async_copy(frame_ref.at[pl.ds(start, half), :], rows, arrived)
    copy.start()
    copy.wait()
    values = rows[...].astype(jnp.float32)
    row_mean = jnp.mean(values, axis=-1, keepdims=True)
    centred = values - row_mean
    row_var = jnp.mean(centred * centred, axis=-1, keepdims=True)
    normed = centred * lax.rsqrt(row_var + 1e-06)
    out_ref[...] = (normed * (1.0 + mod_ref[1:2, :]) + mod_ref[0:1, :]).astype(jnp.bfloat16)


def norm_half(place, frame, modulation):
    half, width = frame.shape[0] // 2, frame.shape[1]
    return call(
        norm_kernel,
        jax.ShapeDtypeStruct((half, width), jnp.bfloat16),
        (place, frame, modulation),
        [pltpu.VMEM((half, width), jnp.bfloat16), pltpu.SemaphoreType.DMA],
        flops=20 * half * width,
        moved=4 * half * width,
        left=(1,),
    )


def weight_kernel(heads, head_dim, group_ref, mine_ref, partner_ref, out_ref):
    parts = []
    for ref in (mine_ref, partner_ref):
        pieces = [ref[source].astype(jnp.float32) for source in range(ref.shape[0])]
        parts.append(jnp.concatenate(pieces, 1))
    swap = group_ref[0] == 1
    per_head = (jnp.where(swap, parts[1], parts[0]), jnp.where(swap, parts[0], parts[1]))
    rows = [w[kind * head_dim : (kind + 1) * head_dim] for kind in (1, 2, 0) for w in per_head]
    out_ref[...] = jnp.concatenate(rows, 0).astype(jnp.bfloat16)


def join_weight(group, mine, partner, heads, head_dim):
    count, part_rows, share = mine.shape
    out = (2 * part_rows, count * share)
    return call(
        functools.partial(weight_kernel, heads, head_dim),
        jax.ShapeDtypeStruct(out, jnp.bfloat16),
        (group, mine, partner),
        flops=4 * out[0] * out[1],
        moved=4 * out[0] * out[1],
    )


def project_kernel(kv_width, sources, *refs):
    pick_ref, weight_ref = refs[0], refs[1]
    pairs = [refs[2 + 2 * i : 4 + 2 * i] for i in range(sources)]
    kv_ref, q_ref, hidden, arrived = refs[2 + 2 * sources :]
    half = pairs[0][0].shape[0]
    starts = (pl.multiple_of(pick_ref[0] * half, half), pl.multiple_of((1 - pick_ref[0]) * half, half))

    def copies(pair):
        return [
            pltpu.make_async_copy(ref, hidden.at[pl.ds(start, half), :], arrived.at[i])
            for i, (ref, start) in enumerate(zip(pair, starts))
        ]

    for i, pair in enumerate(pairs):
        def fetch(pair=pair):
            for copy in copies(pair):
                copy.start()
        if sources == 1:
            fetch()
        else:
            pl.when(pick_ref[1] == i)(fetch)
    for copy in copies(pairs[0]):
        copy.wait()
    mixed = dot_nt(weight_ref[...], hidden[...]).astype(jnp.bfloat16)
    kv_ref[...] = mixed[:kv_width]
    q_ref[...] = mixed[kv_width:]


def project(pick, sources, weight, kv_width):
    half, width = sources[0][0].shape
    rows = 2 * half
    out_width = weight.shape[0]
    flat = [block for pair in sources for block in pair]
    return call(
        functools.partial(project_kernel, kv_width, len(sources)),
        (
            jax.ShapeDtypeStruct((kv_width, rows), jnp.bfloat16),
            jax.ShapeDtypeStruct((out_width - kv_width, rows), jnp.bfloat16),
        ),
        (pick, weight, *flat),
        [pltpu.VMEM((rows, width), jnp.bfloat16), pltpu.SemaphoreType.DMA((2,))],
        flops=2 * rows * width * out_width,
        moved=2 * (rows * width + width * out_width + rows * out_width),
        left=range(2, 2 + len(flat)),
    )


def unpack_queries(ref, frame, heads, head_dim, q_all):
    queries = ref[...].astype(jnp.float32)
    for head in range(heads):
        q_all[frame * heads + head] = queries[head * head_dim : (head + 1) * head_dim].astype(jnp.bfloat16)


def unpack_keyvals(ref, base, side, heads, head_dim, k_all, v_all):
    rows = ref.shape[1]
    ones = jnp.ones((v_all.shape[1] - head_dim, rows), jnp.float32)
    keyvals = ref[...].astype(jnp.float32)
    span = pl.ds(side * rows, rows)
    for head in range(heads):
        keys = keyvals[head * head_dim : (head + 1) * head_dim]
        k_all[base + head, span, :] = keys.T.astype(jnp.bfloat16)
        first = (heads + head) * head_dim
        values = jnp.concatenate([keyvals[first : first + head_dim], ones], 0)
        v_all[base + head, :, span] = values.astype(jnp.bfloat16)


def run_items(items, q_list, k_list, key_rows, heads, head_dim, q_all, k_all, v_all, scores_of, block_high, scale_old, high, total):
    factor = math.log2(math.e) / math.sqrt(head_dim)
    step = math.gcd(key_rows, 256)

    def stage(now, before):
        if now is not None:
            head_a, item_a = now
            state_a = q_list[item_a] * heads + head_a
            key_a = k_list[item_a] * heads + head_a
            queries = q_all[state_a]
            old = high[state_a]
            top = old
        if before is not None:
            head_b, item_b = before
            state_b = q_list[item_b] * heads + head_b
            key_b = k_list[item_b] * heads + head_b
            top_b = block_high[head_b]
            running = total[state_b] * scale_old[head_b]
        for start in range(0, key_rows, step):
            part = pl.ds(start, step)
            if now is not None:
                scores = dot_nn(k_all[key_a, part, :], queries)
                scores_of[head_a][part, :] = scores
                top = jnp.maximum(top, jnp.max(scores, axis=0, keepdims=True))
            if before is not None:
                probs = jnp.exp2((scores_of[head_b][part, :] - top_b) * factor).astype(jnp.bfloat16)
                running = running + dot_nn(v_all[key_b, :, part], probs)
        if before is not None:
            total[state_b] = running
        if now is not None:
            scale_old[head_a] = jnp.exp2((old - top) * factor)
            block_high[head_a] = top
            high[state_a] = top

    def body(index, carry):
        stage((1, index), (0, index))
        stage((0, index + 1), (1, index))
        return carry

    stage((0, 0), None)
    lax.fori_loop(0, items - 1, body, 0)
    stage((1, items - 1), (0, items - 1))
    stage(None, (1, items - 1))


def list_items(count, anchor, keep, q_list, k_list):
    items = jnp.int32(0)
    for frame in range(count):
        pairs = [(jnp.int32(frame), None)]
        if frame > 0:
            pairs.append((jnp.int32(frame - 1), None))
        pairs.append((anchor, (anchor != frame) & (anchor != frame - 1)))
        for key, valid in pairs:
            q_list[items] = frame
            k_list[items] = key
            kept = keep(frame, key)
            items += jnp.where(kept if valid is None else kept & valid, 1, 0)
    return items


def first_kernel(count, heads, head_dim, *refs):
    ids_ref = refs[0]
    q_refs = refs[1 : 1 + count]
    near_refs = refs[1 + count : 1 + 2 * count]
    far_refs = refs[1 + 2 * count : 3 * count]
    high, total = refs[3 * count : 3 * count + 2]
    q_all, k_all, v_all, even, odd, block_high, scale_old, q_list, k_list = refs[3 * count + 2 :]
    rows = q_refs[0].shape[1]
    for slot in range(count):
        frame = ids_ref[slot]
        unpack_queries(q_refs[slot], frame, heads, head_dim, q_all)
        unpack_keyvals(near_refs[slot], frame * heads, 0, heads, head_dim, k_all, v_all)
        if slot < count - 1:
            unpack_keyvals(far_refs[slot], frame * heads, 1, heads, head_dim, k_all, v_all)
    anchor = ids_ref[count]
    late = ids_ref[count - 1]
    high[...] = jnp.full_like(high, -1e30)
    total[...] = jnp.zeros_like(total)
    rest = (heads, head_dim, q_all, k_all, v_all, (even, odd), block_high, scale_old, high, total)
    items = list_items(count, anchor, lambda q, k: k != late, q_list, k_list)
    run_items(items, q_list, k_list, 2 * rows, *rest)
    items = list_items(count, anchor, lambda q, k: k == late, q_list, k_list)
    run_items(items, q_list, k_list, rows, *rest)


def second_kernel(count, heads, head_dim, *refs):
    ids_ref = refs[0]
    q_refs = refs[1 : 1 + count]
    far_ref, high_in, total_in, out_ref = refs[1 + count : 5 + count]
    high, total, q_all, k_late, v_late, even, odd, block_high, scale_old, q_list, k_list = refs[5 + count :]
    rows = q_refs[0].shape[1]
    for slot in range(count):
        unpack_queries(q_refs[slot], ids_ref[slot], heads, head_dim, q_all)
    unpack_keyvals(far_ref, 0, 0, heads, head_dim, k_late, v_late)
    high[...] = high_in[...]
    total[...] = total_in[...]
    late = ids_ref[count - 1]
    items = list_items(count, ids_ref[count], lambda q, k: k == late, q_list, k_list)
    for item in range(count):
        k_list[item] = 0
    run_items(
        items, q_list, k_list, rows, heads, head_dim, q_all, k_late, v_late, (even, odd), block_high, scale_old, high, total
    )
    for frame in range(count):
        parts = []
        for head in range(heads):
            sums = total[frame * heads + head]
            parts.append(sums[:head_dim] / sums[head_dim : head_dim + 1])
        out_ref[frame] = jnp.concatenate(parts, 0).astype(jnp.bfloat16)


def attend_all(ids, queries, near, far, heads, head_dim):
    count = len(queries)
    rows = queries[0].shape[1]
    value_rows = head_dim + 8
    states = count * heads
    f32 = jnp.float32
    lists = [pltpu.SMEM((3 * count + 1,), jnp.int32)] * 2
    tops = [pltpu.VMEM((heads, 1, rows), f32)] * 2
    state = (
        jax.ShapeDtypeStruct((states, 1, rows), f32),
        jax.ShapeDtypeStruct((states, value_rows, rows), f32),
    )
    high, total = call(
        functools.partial(first_kernel, count, heads, head_dim),
        state,
        (ids, *queries, *near, *far[:-1]),
        [
            pltpu.VMEM((states, head_dim, rows), jnp.bfloat16),
            pltpu.VMEM((states, 2 * rows, head_dim), jnp.bfloat16),
            pltpu.VMEM((states, value_rows, 2 * rows), jnp.bfloat16),
            pltpu.VMEM((2 * rows, rows), f32),
            pltpu.VMEM((2 * rows, rows), f32),
            *tops,
            *lists,
        ],
        flops=3 * count * heads * rows * 2 * rows * head_dim * 16,
        moved=2 * count * heads * head_dim * rows * 6,
    )
    return call(
        functools.partial(second_kernel, count, heads, head_dim),
        jax.ShapeDtypeStruct((count, heads * head_dim, rows), jnp.bfloat16),
        (ids, *queries, far[-1], high, total),
        [
            pltpu.VMEM(state[0].shape, f32),
            pltpu.VMEM(state[1].shape, f32),
            pltpu.VMEM((states, head_dim, rows), jnp.bfloat16),
            pltpu.VMEM((heads, rows, head_dim), jnp.bfloat16),
            pltpu.VMEM((heads, value_rows, rows), jnp.bfloat16),
            pltpu.VMEM((rows, rows), f32),
            pltpu.VMEM((rows, rows), f32),
            *tops,
            *lists,
        ],
        flops=heads * rows * rows * head_dim * 16,
        moved=2 * count * heads * head_dim * rows * 6,
    )


def finish_kernel(near_w, far_w, near_ref, far_ref, frame_ref, gate_ref, out_ref):
    projected = dot_nn(near_w[...], near_ref[...]) + dot_nn(far_w[...], far_ref[...])
    updated = frame_ref[...].astype(jnp.float32) + gate_ref[...] * projected
    out_ref[...] = updated.astype(jnp.bfloat16)


def finish(near_w, far_w, near, far, frame_part, gate_part):
    return call(
        finish_kernel,
        jax.ShapeDtypeStruct(frame_part.shape, jnp.bfloat16),
        (near_w, far_w, near, far, frame_part, gate_part),
        flops=4 * near_w.shape[0] * near_w.shape[1] * near.shape[1],
        moved=4 * (near_w.size + near.size + frame_part.size),
    )


def swapped(block, axis):
    return lax.ppermute(block, axis, [(0, 1), (1, 0)])


def shifted(block, axis, distance):
    devices = range(lax.axis_size(axis))
    route = [(i - distance, i) for i in devices if i - distance in devices]
    return lax.ppermute(block, axis, route)


def from_partner(block, axis, stride):
    count = lax.axis_size(axis)
    route = []
    for low in range(count):
        high = low | 1 << stride
        if high != low and high < count:
            route += [(low, high), (high, low)]
    return lax.ppermute(block, axis, route)


def attend(queries, kv_all, first_frame, anchor, head_dim):
    frame_count, query_rows, query_width = queries.shape
    key_count = kv_all.shape[1]
    head_count = query_width // head_dim
    block_rows = math.gcd(512, query_rows)
    kv_heads = kv_all.reshape(frame_count + 2, key_count, head_count, 2, head_dim)
    global_idx = first_frame + 0
    use_prev = global_idx > 0
    use_anchor = (anchor != global_idx) & (anchor != global_idx - 1)
    valid_keys = jnp.concatenate(
        [
            jnp.broadcast_to(use_anchor, (key_count,)),
            jnp.broadcast_to(use_prev, (key_count,)),
            jnp.ones((key_count,), bool),
        ]
    )
    frame_queries = queries[0]

    def one_head(head_idx):
        picked = lax.dynamic_index_in_dim(kv_heads, head_idx, 2, keepdims=False)
        key_rows = jnp.concatenate(
            [picked[frame_count + 1, :, 0], picked[frame_count, :, 0], picked[0, :, 0]], 0
        )
        val_rows = jnp.concatenate(
            [picked[frame_count + 1, :, 1], picked[frame_count, :, 1], picked[0, :, 1]], 0
        )
        query_head = lax.dynamic_slice_in_dim(frame_queries, head_idx * head_dim, head_dim, 1)
        query_blocks = query_head.reshape(query_rows // block_rows, block_rows, head_dim)

        def one_block(query_block):
            scores = lax.dot_general(
                query_block, key_rows, (((1,), (1,)), ((), ())), preferred_element_type=jnp.float32
            ) * head_dim ** (-0.5)
            scores = jnp.where(valid_keys[None, :], scores, -1e30)
            row_max = jnp.max(scores, axis=-1, keepdims=True)
            probs = jnp.exp(scores - row_max)
            denominator = jnp.sum(probs, axis=-1, keepdims=True)
            numerator = jnp.dot(
                probs.astype(jnp.bfloat16), val_rows, preferred_element_type=jnp.float32
            )
            return (numerator / denominator).astype(jnp.bfloat16)

        return lax.map(one_block, query_blocks).reshape(query_rows, head_dim)

    per_head = lax.map(one_head, jnp.arange(head_count, dtype=jnp.int32))
    frame_outputs = [jnp.transpose(per_head, (1, 0, 2)).reshape(query_rows, head_count * head_dim)]
    return jnp.stack(frame_outputs)


def by_frames(frames, modulation, w_qkv, w_out, anchor_offsets):
    frame_count, row_count, model_width = frames.shape
    head_local = w_qkv.shape[1]
    head_dim = w_qkv.shape[3]
    my_index = lax.axis_index("frame")
    flat_rows = frames.reshape(frame_count * row_count, model_width).astype(jnp.float32)
    row_mean = jnp.mean(flat_rows, axis=-1, keepdims=True)
    centred = flat_rows - row_mean
    row_var = jnp.mean(centred * centred, axis=-1, keepdims=True)
    normed = centred * lax.rsqrt(row_var + 1e-06)
    hidden = (normed * (1.0 + modulation[1]) + modulation[0]).astype(jnp.bfloat16)
    full_weight = lax.all_gather(w_qkv, "frame", axis=0, tiled=True)
    mixed = jnp.dot(
        hidden,
        full_weight.reshape(model_width, head_local * 3 * head_dim),
        preferred_element_type=jnp.float32,
    )
    mixed = mixed.astype(jnp.bfloat16).reshape(frame_count, row_count, head_local, 3, head_dim)
    queries = mixed[:, :, :, 0, :].reshape(frame_count, row_count, head_local * head_dim)
    keyvals = mixed[:, :, :, 1:, :].reshape(frame_count, row_count, head_local * 2 * head_dim)
    span_count = anchor_offsets.shape[0]
    total_frames = frame_count * lax.axis_size("frame")
    span_len = total_frames // span_count
    first_frame = my_index * frame_count
    mine_span = first_frame // span_len
    anchor = mine_span * span_len + anchor_offsets[mine_span]
    prev_kv = shifted(keyvals[frame_count - 1], "frame", 1)
    holder = anchor // frame_count
    anchor_kv = lax.dynamic_index_in_dim(keyvals, anchor % frame_count, 0, keepdims=False)
    levels = (span_len // frame_count).bit_length() - 1
    for bit_index in range(levels):
        partner = from_partner(anchor_kv, "frame", bit_index)
        take_partner = my_index >> bit_index & 1 != holder >> bit_index & 1
        anchor_kv = jnp.where(take_partner, partner, anchor_kv)
    kv_all = jnp.concatenate([keyvals, prev_kv[None], anchor_kv[None]], 0)
    kv_whole = lax.all_gather(kv_all, "tok", axis=1, tiled=True)
    attended = attend(queries, kv_whole, first_frame, anchor, head_dim)
    flat_attended = attended.reshape(frame_count * row_count, head_local * head_dim)
    term_cols = jnp.dot(
        flat_attended,
        lax.all_gather(w_out, "frame", axis=1, tiled=True),
        preferred_element_type=jnp.float32,
    )
    summed = lax.psum_scatter(term_cols, "head", scatter_dimension=1, tiled=True)
    half_width = summed.shape[1]
    col_start = lax.axis_index("head") * half_width
    residual_in = lax.dynamic_slice_in_dim(flat_rows, col_start, half_width, 1)
    gate_part = lax.dynamic_slice_in_dim(modulation[2], col_start, half_width, 0)
    result = (residual_in + gate_part * summed).astype(jnp.bfloat16)
    return result.reshape(frame_count, row_count, half_width)


def after(block, other):
    return lax.optimization_barrier((block, other))[0]


def by_heads(frames, modulation, w_qkv, w_out, anchor_offsets):
    _, rows, width = frames.shape
    share, head_local, _, head_dim = w_qkv.shape
    count = lax.axis_size("frame")
    heads = head_local // count
    core = lax.axis_index("head")
    me = lax.axis_index("frame")
    group = lax.axis_index("groups")
    frame = frames[0]
    place = core.reshape(1).astype(jnp.int32)
    middle = count // 2

    blocks = jnp.transpose(w_qkv, (1, 2, 3, 0)).reshape(count, heads, 3 * head_dim, share)
    part = lax.dynamic_index_in_dim(blocks, group, 1, keepdims=False)
    part = lax.all_to_all(part, "frame", 0, 0)
    weight = join_weight(group.reshape(1).astype(jnp.int32), part, swapped(part, "groups"), heads, head_dim)
    kv_width = 2 * heads * head_dim

    mine = norm_half(place, frame, modulation)
    across = lax.ppermute(mine, "frame", [(i, i ^ middle) for i in range(count)])
    right = lax.ppermute(mine, "frame", [(i, i + 1) for i in range(count - 1)])
    left = lax.ppermute(mine, "frame", [(i + 1, i) for i in range(count - 1)])
    ends = lax.ppermute(across, "frame", [(count - 2, count - 1), (1, 0)])
    pairs = {name: (block, swapped(block, "head")) for name, block in (("own", mine), ("right", right), ("left", left), ("across", across), ("ends", ends))}

    at_end = (me == 0) | (me == count - 1)
    slots = (
        (me, 0, ("own",)),
        (jnp.where(me == 0, 1, me - 1), jnp.where(me == 0, 1, 0), ("right", "left")),
        (me ^ middle, 0, ("across",)),
        (jnp.where(at_end, count - 1 - me, me + 1), jnp.where(at_end, 1, 0), ("left", "ends")),
    )
    queries, near, far = [], [], []
    for _, pick, names in slots:
        picked = jnp.stack([core, pick]).astype(jnp.int32)
        kv, q = project(picked, [pairs[name] for name in names], weight, kv_width)
        queries.append(q)
        near.append(kv)
        far.append(swapped(kv, "tok"))
    ids = jnp.stack([index for index, _, _ in slots] + [anchor_offsets[0]]).astype(jnp.int32)
    attended = attend_all(ids, queries, near, far, heads, head_dim)
    arrived = lax.all_to_all(attended, "frame", 0, 0).reshape(count * heads * head_dim, rows)
    arrived_far = swapped(arrived, "head")

    out_half = width // 2
    columns = w_out.shape[1] // 2
    w_part = lax.dynamic_slice_in_dim(w_out.T, group * columns, columns, 0)
    w_part = after(w_part, ends)
    w_part = lax.all_to_all(jnp.broadcast_to(w_part[None], (count, *w_part.shape)), "frame", 0, 0)
    w_other = swapped(w_part, "groups")
    w_first = jnp.where(group == 0, w_part, w_other)
    w_second = jnp.where(group == 0, w_other, w_part)
    w_cols = jnp.concatenate([w_first, w_second], 1).reshape(width, w_out.shape[0])
    near_w = lax.dynamic_slice_in_dim(w_cols, core * out_half, out_half, 0)
    far_w = swapped(lax.dynamic_slice_in_dim(w_cols, (1 - core) * out_half, out_half, 0), "head")
    frame_part = lax.dynamic_slice_in_dim(frame, core * out_half, out_half, 1).T
    gate_part = lax.dynamic_slice_in_dim(modulation[2], core * out_half, out_half, 0)[:, None]
    updated = finish(near_w, far_w, arrived, arrived_far, frame_part, gate_part)
    return updated.T[None]


def on_device(frames, modulation, w_qkv, w_out, anchor_offsets):
    count = lax.axis_size("frame")
    fits = (
        frames.shape[0] == 1
        and anchor_offsets.shape[0] == 1
        and count == 4
        and lax.axis_size("groups") == 2
        and lax.axis_size("head") == 2
        and lax.axis_size("tok") == 2
        and w_qkv.shape[1] == 2 * count
        and w_qkv.shape[3] % 8 == 0
        and frames.shape[1] % 256 == 0
        and frames.shape[2] % 32 == 0
    )
    step = by_heads if fits else by_frames
    return step(frames, modulation, w_qkv, w_out, anchor_offsets)


def solution(mesh):
    placed = (
        P(("groups", "frame"), "tok", None),
        P(),
        P("frame", "head", None, None),
        P("head", "frame"),
        P("groups"),
    )
    return jax.shard_map(
        on_device,
        mesh=mesh,
        in_specs=placed,
        out_specs=P(("groups", "frame"), "tok", "head"),
        check_vma=False,
    )
```

```python
import functools
import math

import jax
import jax.numpy as jnp
from jax import lax
from jax.experimental import pallas as pl
from jax.experimental.pallas import tpu as pltpu
from jax.sharding import PartitionSpec as P

MIB = 2**20


def dot_nn(a, b):
    return lax.dot_general(a, b, (((1,), (0,)), ((), ())), preferred_element_type=jnp.float32)


def dot_nt(a, b):
    return lax.dot_general(a, b, (((1,), (1,)), ((), ())), preferred_element_type=jnp.float32)


def call(kernel, out_shape, operands, scratch=(), flops=0, moved=0, left=(), grant=8):
    smem = pl.BlockSpec(memory_space=pltpu.SMEM)
    vmem = pl.BlockSpec(memory_space=pltpu.VMEM)
    where = pl.BlockSpec(memory_space=pl.ANY)
    many = isinstance(out_shape, (list, tuple))
    return pl.pallas_call(
        kernel,
        out_shape=out_shape,
        in_specs=[where if i in left else smem if x.dtype == jnp.int32 else vmem for i, x in enumerate(operands)],
        out_specs=[vmem] * len(out_shape) if many else vmem,
        scratch_shapes=list(scratch),
        compiler_params=pltpu.CompilerParams(vmem_limit_bytes=grant * MIB),
        cost_estimate=pl.CostEstimate(flops=flops, bytes_accessed=moved, transcendentals=0),
    )(*operands)


def norm_kernel(place_ref, frame_ref, mod_ref, out_ref, rows, arrived):
    half = out_ref.shape[0]
    start = pl.multiple_of(place_ref[0] * half, half)
    copy = pltpu.make_async_copy(frame_ref.at[pl.ds(start, half), :], rows, arrived)
    copy.start()
    copy.wait()
    values = rows[...].astype(jnp.float32)
    row_mean = jnp.mean(values, axis=-1, keepdims=True)
    centred = values - row_mean
    row_var = jnp.mean(centred * centred, axis=-1, keepdims=True)
    normed = centred * lax.rsqrt(row_var + 1e-06)
    out_ref[...] = (normed * (1.0 + mod_ref[1:2, :]) + mod_ref[0:1, :]).astype(jnp.bfloat16)


def norm_half(place, frame, modulation):
    half, width = frame.shape[0] // 2, frame.shape[1]
    return call(
        norm_kernel,
        jax.ShapeDtypeStruct((half, width), jnp.bfloat16),
        (place, frame, modulation),
        [pltpu.VMEM((half, width), jnp.bfloat16), pltpu.SemaphoreType.DMA],
        flops=20 * half * width,
        moved=4 * half * width,
        left=(1,),
    )


def weight_kernel(heads, head_dim, parts_ref, out_ref):
    _, count, part_rows, share = parts_ref.shape
    head_rows = 3 * head_dim
    per_head = []
    for head in range(heads):
        low, high = [
            jnp.concatenate([parts_ref[head * 2 + i, source].astype(jnp.float32) for source in range(count)], 1)
            for i in range(2)
        ]
        per_head.append(jnp.concatenate([low, high[2 * part_rows - head_rows :]], 0))
    rows = [w[kind * head_dim : (kind + 1) * head_dim] for kind in (1, 2, 0) for w in per_head]
    out_ref[...] = jnp.concatenate(rows, 0).astype(jnp.bfloat16)


def join_weight(parts, heads, head_dim):
    _, count, _, share = parts.shape
    out = (heads * 3 * head_dim, count * share)
    return call(
        functools.partial(weight_kernel, heads, head_dim),
        jax.ShapeDtypeStruct(out, jnp.bfloat16),
        (parts,),
        flops=4 * out[0] * out[1],
        moved=4 * out[0] * out[1],
        grant=16,
    )


def project_kernel(kv_width, place_ref, weight_ref, mine_ref, other_ref, kv_ref, q_ref):
    half = mine_ref.shape[0]
    for part, ref in ((place_ref[0], mine_ref), (1 - place_ref[0], other_ref)):
        span = pl.ds(pl.multiple_of(part * half, half), half)
        mixed = dot_nt(weight_ref[...], ref[...]).astype(jnp.bfloat16)
        kv_ref[:, span] = mixed[:kv_width]
        q_ref[:, span] = mixed[kv_width:]


def project(place, weight, mine, other, kv_width):
    half, width = mine.shape
    rows = 2 * half
    out_width = weight.shape[0]
    return call(
        functools.partial(project_kernel, kv_width),
        (
            jax.ShapeDtypeStruct((kv_width, rows), jnp.bfloat16),
            jax.ShapeDtypeStruct((out_width - kv_width, rows), jnp.bfloat16),
        ),
        (place, weight, mine, other),
        flops=2 * rows * width * out_width,
        moved=2 * (rows * width + width * out_width + rows * out_width),
    )


def unpack_queries(ref, frame, heads, head_dim, q_all):
    queries = ref[...].astype(jnp.float32)
    for head in range(heads):
        q_all[frame * heads + head] = queries[head * head_dim : (head + 1) * head_dim].astype(jnp.bfloat16)


def unpack_keyvals(ref, base, side, heads, head_dim, k_all, v_all):
    rows = ref.shape[1]
    ones = jnp.ones((v_all.shape[1] - head_dim, rows), jnp.float32)
    keyvals = ref[...].astype(jnp.float32)
    span = pl.ds(side * rows, rows)
    for head in range(heads):
        keys = keyvals[head * head_dim : (head + 1) * head_dim]
        k_all[base + head, span, :] = keys.T.astype(jnp.bfloat16)
        first = (heads + head) * head_dim
        values = jnp.concatenate([keyvals[first : first + head_dim], ones], 0)
        v_all[base + head, :, span] = values.astype(jnp.bfloat16)


def run_items(items, q_list, k_list, key_rows, heads, head_dim, q_all, k_all, v_all, scores_of, block_high, scale_old, high, total):
    factor = math.log2(math.e) / math.sqrt(head_dim)
    step = math.gcd(key_rows, 256)

    def stage(now, before):
        if now is not None:
            head_a, item_a = now
            state_a = q_list[item_a] * heads + head_a
            key_a = k_list[item_a] * heads + head_a
            queries = q_all[state_a]
            old = high[state_a]
            top = old
        if before is not None:
            head_b, item_b = before
            state_b = q_list[item_b] * heads + head_b
            key_b = k_list[item_b] * heads + head_b
            top_b = block_high[head_b]
            running = total[state_b] * scale_old[head_b]
        for start in range(0, key_rows, step):
            part = pl.ds(start, step)
            if now is not None:
                scores = dot_nn(k_all[key_a, part, :], queries)
                scores_of[head_a][part, :] = scores
                top = jnp.maximum(top, jnp.max(scores, axis=0, keepdims=True))
            if before is not None:
                probs = jnp.exp2((scores_of[head_b][part, :] - top_b) * factor).astype(jnp.bfloat16)
                running = running + dot_nn(v_all[key_b, :, part], probs)
        if before is not None:
            total[state_b] = running
        if now is not None:
            scale_old[head_a] = jnp.exp2((old - top) * factor)
            block_high[head_a] = top
            high[state_a] = top

    def body(index, carry):
        stage((1, index), (0, index))
        stage((0, index + 1), (1, index))
        return carry

    stage((0, 0), None)
    lax.fori_loop(0, items - 1, body, 0)
    stage((1, items - 1), (0, items - 1))
    stage(None, (1, items - 1))


def list_items(count, anchor, keep, q_list, k_list):
    items = jnp.int32(0)
    for frame in range(count):
        pairs = [(jnp.int32(frame), None)]
        if frame > 0:
            pairs.append((jnp.int32(frame - 1), None))
        pairs.append((anchor, (anchor != frame) & (anchor != frame - 1)))
        for key, valid in pairs:
            q_list[items] = frame
            k_list[items] = key
            kept = keep(frame, key)
            items += jnp.where(kept if valid is None else kept & valid, 1, 0)
    return items


def first_kernel(count, heads, head_dim, *refs):
    ids_ref = refs[0]
    q_refs = refs[1 : 1 + count]
    near_refs = refs[1 + count : 1 + 2 * count]
    far_refs = refs[1 + 2 * count : 3 * count]
    high, total = refs[3 * count : 3 * count + 2]
    q_all, k_all, v_all, even, odd, block_high, scale_old, q_list, k_list = refs[3 * count + 2 :]
    rows = q_refs[0].shape[1]
    for slot in range(count):
        frame = ids_ref[slot]
        unpack_queries(q_refs[slot], frame, heads, head_dim, q_all)
        unpack_keyvals(near_refs[slot], frame * heads, 0, heads, head_dim, k_all, v_all)
        if slot < count - 1:
            unpack_keyvals(far_refs[slot], frame * heads, 1, heads, head_dim, k_all, v_all)
    anchor = ids_ref[count]
    late = ids_ref[count - 1]
    high[...] = jnp.full_like(high, -1e30)
    total[...] = jnp.zeros_like(total)
    rest = (heads, head_dim, q_all, k_all, v_all, (even, odd), block_high, scale_old, high, total)
    items = list_items(count, anchor, lambda q, k: k != late, q_list, k_list)
    run_items(items, q_list, k_list, 2 * rows, *rest)
    items = list_items(count, anchor, lambda q, k: k == late, q_list, k_list)
    run_items(items, q_list, k_list, rows, *rest)


def second_kernel(count, heads, head_dim, *refs):
    ids_ref = refs[0]
    q_refs = refs[1 : 1 + count]
    far_ref, high_in, total_in, out_ref = refs[1 + count : 5 + count]
    high, total, q_all, k_late, v_late, even, odd, block_high, scale_old, q_list, k_list = refs[5 + count :]
    rows = q_refs[0].shape[1]
    for slot in range(count):
        unpack_queries(q_refs[slot], ids_ref[slot], heads, head_dim, q_all)
    unpack_keyvals(far_ref, 0, 0, heads, head_dim, k_late, v_late)
    high[...] = high_in[...]
    total[...] = total_in[...]
    late = ids_ref[count - 1]
    items = list_items(count, ids_ref[count], lambda q, k: k == late, q_list, k_list)
    for item in range(count):
        k_list[item] = 0
    run_items(
        items, q_list, k_list, rows, heads, head_dim, q_all, k_late, v_late, (even, odd), block_high, scale_old, high, total
    )
    for frame in range(count):
        parts = []
        for head in range(heads):
            sums = total[frame * heads + head]
            parts.append(sums[:head_dim] / sums[head_dim : head_dim + 1])
        out_ref[frame] = jnp.concatenate(parts, 0).astype(jnp.bfloat16)


def attend_all(ids, queries, near, far, heads, head_dim):
    count = len(queries)
    rows = queries[0].shape[1]
    value_rows = head_dim + 8
    states = count * heads
    f32 = jnp.float32
    lists = [pltpu.SMEM((3 * count + 1,), jnp.int32)] * 2
    tops = [pltpu.VMEM((heads, 1, rows), f32)] * 2
    state = (
        jax.ShapeDtypeStruct((states, 1, rows), f32),
        jax.ShapeDtypeStruct((states, value_rows, rows), f32),
    )
    high, total = call(
        functools.partial(first_kernel, count, heads, head_dim),
        state,
        (ids, *queries, *near, *far[:-1]),
        [
            pltpu.VMEM((states, head_dim, rows), jnp.bfloat16),
            pltpu.VMEM((states, 2 * rows, head_dim), jnp.bfloat16),
            pltpu.VMEM((states, value_rows, 2 * rows), jnp.bfloat16),
            pltpu.VMEM((2 * rows, rows), f32),
            pltpu.VMEM((2 * rows, rows), f32),
            *tops,
            *lists,
        ],
        flops=3 * count * heads * rows * 2 * rows * head_dim * 16,
        moved=2 * count * heads * head_dim * rows * 6,
        grant=24,
    )
    return call(
        functools.partial(second_kernel, count, heads, head_dim),
        jax.ShapeDtypeStruct((count, heads * head_dim, rows), jnp.bfloat16),
        (ids, *queries, far[-1], high, total),
        [
            pltpu.VMEM(state[0].shape, f32),
            pltpu.VMEM(state[1].shape, f32),
            pltpu.VMEM((states, head_dim, rows), jnp.bfloat16),
            pltpu.VMEM((heads, rows, head_dim), jnp.bfloat16),
            pltpu.VMEM((heads, value_rows, rows), jnp.bfloat16),
            pltpu.VMEM((rows, rows), f32),
            pltpu.VMEM((rows, rows), f32),
            *tops,
            *lists,
        ],
        flops=heads * rows * rows * head_dim * 16,
        moved=2 * count * heads * head_dim * rows * 6,
        grant=16,
    )


def residual_kernel(core_ref, frame_ref, mod_ref, out_ref, gate_ref):
    width = out_ref.shape[0]
    frame = frame_ref[...].astype(jnp.float32)
    mine = jnp.where(core_ref[0] == 0, frame[:, :width], frame[:, width:])
    out_ref[...] = mine.T.astype(jnp.bfloat16)
    gate = jnp.broadcast_to(mod_ref[2:3, :], (8, 2 * width))
    gate = jnp.where(core_ref[0] == 0, gate[:, :width], gate[:, width:])
    gate_ref[...] = gate.T


def residual(core, frame, modulation):
    rows, width = frame.shape
    return call(
        residual_kernel,
        (jax.ShapeDtypeStruct((width // 2, rows), jnp.bfloat16), jax.ShapeDtypeStruct((width // 2, 8), jnp.float32)),
        (core, frame, modulation),
        flops=4 * rows * width,
        moved=3 * rows * width,
        grant=16,
    )


def order_kernel(where_ref, mine_ref, other_ref, near_ref, send_ref):
    group, core = where_ref[1], where_ref[3]
    block = mine_ref.shape[1]
    per_core = mine_ref.shape[0] // 2
    for same, ref in ((True, mine_ref), (False, other_ref)):
        half = group if same else 1 - group
        for index in range(per_core):
            start = pl.multiple_of((index * 2 + half) * block, block)
            near_ref[pl.ds(start, block), :] = ref[core * per_core + index]
            send_ref[pl.ds(start, block), :] = ref[(1 - core) * per_core + index]


def order_columns(where, mine, other):
    count, block, depth = mine.shape
    out = jax.ShapeDtypeStruct((count * block, depth), mine.dtype)
    return call(order_kernel, (out, out), (where, mine, other), moved=8 * mine.size, grant=8)


def finish_kernel(near_w, far_w, near_ref, far_ref, frame_ref, gate_ref, out_ref):
    projected = dot_nn(near_w[...], near_ref[...]) + dot_nn(far_w[...], far_ref[...])
    updated = frame_ref[...].astype(jnp.float32) + gate_ref[:, 0:1] * projected
    out_ref[...] = updated.astype(jnp.bfloat16)


def finish(near_w, far_w, near, far, frame_part, gate_part):
    return call(
        finish_kernel,
        jax.ShapeDtypeStruct(frame_part.shape, jnp.bfloat16),
        (near_w, far_w, near, far, frame_part, gate_part),
        flops=4 * near_w.shape[0] * near_w.shape[1] * near.shape[1],
        moved=4 * (near_w.size + near.size + frame_part.size),
        grant=16,
    )


def swapped(block, axis):
    return lax.ppermute(block, axis, [(0, 1), (1, 0)])


def shifted(block, axis, distance):
    devices = range(lax.axis_size(axis))
    route = [(i - distance, i) for i in devices if i - distance in devices]
    return lax.ppermute(block, axis, route)


def from_partner(block, axis, stride):
    count = lax.axis_size(axis)
    route = []
    for low in range(count):
        high = low | 1 << stride
        if high != low and high < count:
            route += [(low, high), (high, low)]
    return lax.ppermute(block, axis, route)


def attend(queries, kv_all, first_frame, anchor, head_dim):
    frame_count, query_rows, query_width = queries.shape
    key_count = kv_all.shape[1]
    head_count = query_width // head_dim
    block_rows = math.gcd(512, query_rows)
    kv_heads = kv_all.reshape(frame_count + 2, key_count, head_count, 2, head_dim)
    global_idx = first_frame + 0
    use_prev = global_idx > 0
    use_anchor = (anchor != global_idx) & (anchor != global_idx - 1)
    valid_keys = jnp.concatenate(
        [
            jnp.broadcast_to(use_anchor, (key_count,)),
            jnp.broadcast_to(use_prev, (key_count,)),
            jnp.ones((key_count,), bool),
        ]
    )
    frame_queries = queries[0]

    def one_head(head_idx):
        picked = lax.dynamic_index_in_dim(kv_heads, head_idx, 2, keepdims=False)
        key_rows = jnp.concatenate(
            [picked[frame_count + 1, :, 0], picked[frame_count, :, 0], picked[0, :, 0]], 0
        )
        val_rows = jnp.concatenate(
            [picked[frame_count + 1, :, 1], picked[frame_count, :, 1], picked[0, :, 1]], 0
        )
        query_head = lax.dynamic_slice_in_dim(frame_queries, head_idx * head_dim, head_dim, 1)
        query_blocks = query_head.reshape(query_rows // block_rows, block_rows, head_dim)

        def one_block(query_block):
            scores = lax.dot_general(
                query_block, key_rows, (((1,), (1,)), ((), ())), preferred_element_type=jnp.float32
            ) * head_dim ** (-0.5)
            scores = jnp.where(valid_keys[None, :], scores, -1e30)
            row_max = jnp.max(scores, axis=-1, keepdims=True)
            probs = jnp.exp(scores - row_max)
            denominator = jnp.sum(probs, axis=-1, keepdims=True)
            numerator = jnp.dot(
                probs.astype(jnp.bfloat16), val_rows, preferred_element_type=jnp.float32
            )
            return (numerator / denominator).astype(jnp.bfloat16)

        return lax.map(one_block, query_blocks).reshape(query_rows, head_dim)

    per_head = lax.map(one_head, jnp.arange(head_count, dtype=jnp.int32))
    frame_outputs = [jnp.transpose(per_head, (1, 0, 2)).reshape(query_rows, head_count * head_dim)]
    return jnp.stack(frame_outputs)


def by_frames(frames, modulation, w_qkv, w_out, anchor_offsets):
    frame_count, row_count, model_width = frames.shape
    head_local = w_qkv.shape[1]
    head_dim = w_qkv.shape[3]
    my_index = lax.axis_index("frame")
    flat_rows = frames.reshape(frame_count * row_count, model_width).astype(jnp.float32)
    row_mean = jnp.mean(flat_rows, axis=-1, keepdims=True)
    centred = flat_rows - row_mean
    row_var = jnp.mean(centred * centred, axis=-1, keepdims=True)
    normed = centred * lax.rsqrt(row_var + 1e-06)
    hidden = (normed * (1.0 + modulation[1]) + modulation[0]).astype(jnp.bfloat16)
    full_weight = lax.all_gather(w_qkv, "frame", axis=0, tiled=True)
    mixed = jnp.dot(
        hidden,
        full_weight.reshape(model_width, head_local * 3 * head_dim),
        preferred_element_type=jnp.float32,
    )
    mixed = mixed.astype(jnp.bfloat16).reshape(frame_count, row_count, head_local, 3, head_dim)
    queries = mixed[:, :, :, 0, :].reshape(frame_count, row_count, head_local * head_dim)
    keyvals = mixed[:, :, :, 1:, :].reshape(frame_count, row_count, head_local * 2 * head_dim)
    span_count = anchor_offsets.shape[0]
    total_frames = frame_count * lax.axis_size("frame")
    span_len = total_frames // span_count
    first_frame = my_index * frame_count
    mine_span = first_frame // span_len
    anchor = mine_span * span_len + anchor_offsets[mine_span]
    prev_kv = shifted(keyvals[frame_count - 1], "frame", 1)
    holder = anchor // frame_count
    anchor_kv = lax.dynamic_index_in_dim(keyvals, anchor % frame_count, 0, keepdims=False)
    levels = (span_len // frame_count).bit_length() - 1
    for bit_index in range(levels):
        partner = from_partner(anchor_kv, "frame", bit_index)
        take_partner = my_index >> bit_index & 1 != holder >> bit_index & 1
        anchor_kv = jnp.where(take_partner, partner, anchor_kv)
    kv_all = jnp.concatenate([keyvals, prev_kv[None], anchor_kv[None]], 0)
    kv_whole = lax.all_gather(kv_all, "tok", axis=1, tiled=True)
    attended = attend(queries, kv_whole, first_frame, anchor, head_dim)
    flat_attended = attended.reshape(frame_count * row_count, head_local * head_dim)
    term_cols = jnp.dot(
        flat_attended,
        lax.all_gather(w_out, "frame", axis=1, tiled=True),
        preferred_element_type=jnp.float32,
    )
    summed = lax.psum_scatter(term_cols, "head", scatter_dimension=1, tiled=True)
    half_width = summed.shape[1]
    col_start = lax.axis_index("head") * half_width
    residual_in = lax.dynamic_slice_in_dim(flat_rows, col_start, half_width, 1)
    gate_part = lax.dynamic_slice_in_dim(modulation[2], col_start, half_width, 0)
    result = (residual_in + gate_part * summed).astype(jnp.bfloat16)
    return result.reshape(frame_count, row_count, half_width)


def flipped(block, axis, distance):
    return lax.ppermute(block, axis, [(i, i ^ distance) for i in range(lax.axis_size(axis))])


def after(block, other):
    return lax.optimization_barrier((block, other))[0]


def by_heads(frames, modulation, w_qkv, w_out, anchor_offsets):
    _, rows, width = frames.shape
    share, head_local, _, head_dim = w_qkv.shape
    count = lax.axis_size("frame")
    heads = head_local // count
    core = lax.axis_index("head")
    me = lax.axis_index("frame")
    group = lax.axis_index("groups")
    frame = frames[0]
    place = core.reshape(1).astype(jnp.int32)

    tok = lax.axis_index("tok")
    where = jnp.stack([me, group, tok, core]).astype(jnp.int32)

    blocks = jnp.transpose(w_qkv, (1, 2, 3, 0)).reshape(count, heads, 3 * head_dim, share)
    part_rows = -(-3 * head_dim // 32) * 16
    start = tok * (3 * head_dim - part_rows)
    part = lax.dynamic_slice(blocks, (0, group, start, 0), (count, 1, part_rows, share))[:, 0]
    part = lax.all_to_all(part, "frame", 0, 0)
    plane = lax.all_to_all(jnp.broadcast_to(part[None], (4, *part.shape)), ("groups", "tok"), 0, 0)
    weight = join_weight(plane, heads, head_dim)
    kv_width = 2 * heads * head_dim

    mine = norm_half(place, frame, modulation)
    arrivals = [mine, flipped(mine, "frame", 1), flipped(mine, "frame", 2)]
    arrivals.append(flipped(arrivals[2], "frame", 1))
    frame_part, gate_part = residual(place, after(frame, arrivals[1]), modulation)

    queries, near, far = [], [], []
    for distance, block in enumerate(arrivals):
        if distance == 3:
            block = after(block, (frame_part, near[0], near[1]))
        kv, q = project(place, weight, block, swapped(block, "head"), kv_width)
        queries.append(q)
        near.append(kv)
        far.append(swapped(kv, "tok"))
    ids = jnp.stack([me ^ distance for distance in range(count)] + [anchor_offsets[0]]).astype(jnp.int32)
    attended = attend_all(ids, queries, near, far, heads, head_dim)
    arrived = lax.all_to_all(attended, "frame", 0, 0).reshape(count * heads * head_dim, rows)
    arrived_far = swapped(arrived, "head")

    columns = w_out.shape[1] // 2
    w_part = lax.dynamic_slice_in_dim(w_out.T, group * columns, columns, 0)
    w_part = after(w_part, near[-1])
    w_part = lax.all_to_all(jnp.broadcast_to(w_part[None], (count, *w_part.shape)), "frame", 0, 0)
    near_w, send_w = order_columns(where, w_part, swapped(w_part, "groups"))
    far_w = swapped(send_w, "head")
    updated = finish(near_w, far_w, arrived, arrived_far, frame_part, gate_part)
    return updated.T[None]


def on_device(frames, modulation, w_qkv, w_out, anchor_offsets):
    count = lax.axis_size("frame")
    fits = (
        frames.shape[0] == 1
        and anchor_offsets.shape[0] == 1
        and count == 4
        and lax.axis_size("groups") == 2
        and lax.axis_size("head") == 2
        and lax.axis_size("tok") == 2
        and w_qkv.shape[1] == 2 * count
        and w_qkv.shape[3] % 8 == 0
        and frames.shape[1] % 256 == 0
        and frames.shape[2] % 32 == 0
    )
    step = by_heads if fits else by_frames
    return step(frames, modulation, w_qkv, w_out, anchor_offsets)


def solution(mesh):
    placed = (
        P(("groups", "frame"), "tok", None),
        P(),
        P("frame", "head", None, None),
        P("head", "frame"),
        P("groups"),
    )
    return jax.shard_map(
        on_device,
        mesh=mesh,
        in_specs=placed,
        out_specs=P(("groups", "frame"), "tok", "head"),
        check_vma=False,
    )
```

```python
import functools
import math

import jax
import jax.numpy as jnp
from jax import lax
from jax.experimental import pallas as pl
from jax.experimental.pallas import tpu as pltpu
from jax.sharding import PartitionSpec as P

MIB = 2**20


def dot_nn(a, b):
    return lax.dot_general(a, b, (((1,), (0,)), ((), ())), preferred_element_type=jnp.float32)


def dot_nt(a, b):
    return lax.dot_general(a, b, (((1,), (1,)), ((), ())), preferred_element_type=jnp.float32)


def call(kernel, out_shape, operands, scratch=(), flops=0, moved=0, left=(), grant=8):
    smem = pl.BlockSpec(memory_space=pltpu.SMEM)
    vmem = pl.BlockSpec(memory_space=pltpu.VMEM)
    where = pl.BlockSpec(memory_space=pl.ANY)
    many = isinstance(out_shape, (list, tuple))
    return pl.pallas_call(
        kernel,
        out_shape=out_shape,
        in_specs=[where if i in left else smem if x.dtype == jnp.int32 else vmem for i, x in enumerate(operands)],
        out_specs=[vmem] * len(out_shape) if many else vmem,
        scratch_shapes=list(scratch),
        compiler_params=pltpu.CompilerParams(vmem_limit_bytes=grant * MIB),
        cost_estimate=pl.CostEstimate(flops=flops, bytes_accessed=moved, transcendentals=0),
    )(*operands)


def norm_kernel(place_ref, frame_ref, mod_ref, out_ref, rows, arrived):
    half = out_ref.shape[0]
    start = pl.multiple_of(place_ref[0] * half, half)
    copy = pltpu.make_async_copy(frame_ref.at[pl.ds(start, half), :], rows, arrived)
    copy.start()
    copy.wait()
    values = rows[...].astype(jnp.float32)
    row_mean = jnp.mean(values, axis=-1, keepdims=True)
    centred = values - row_mean
    row_var = jnp.mean(centred * centred, axis=-1, keepdims=True)
    normed = centred * lax.rsqrt(row_var + 1e-06)
    out_ref[...] = (normed * (1.0 + mod_ref[1:2, :]) + mod_ref[0:1, :]).astype(jnp.bfloat16)


def norm_half(place, frame, modulation):
    half, width = frame.shape[0] // 2, frame.shape[1]
    return call(
        norm_kernel,
        jax.ShapeDtypeStruct((half, width), jnp.bfloat16),
        (place, frame, modulation),
        [pltpu.VMEM((half, width), jnp.bfloat16), pltpu.SemaphoreType.DMA],
        flops=20 * half * width,
        moved=4 * half * width,
        left=(1,),
    )


def weight_kernel(heads, head_dim, parts_ref, out_ref):
    _, count, share, part_rows = parts_ref.shape
    head_rows = 3 * head_dim
    per_head = []
    for head in range(heads):
        low, high = [
            jnp.concatenate([parts_ref[head * 2 + i, source] for source in range(count)], 0).astype(jnp.float32).T
            for i in range(2)
        ]
        per_head.append(jnp.concatenate([low, high[2 * part_rows - head_rows :]], 0))
    rows = [w[kind * head_dim : (kind + 1) * head_dim] for kind in (1, 2, 0) for w in per_head]
    out_ref[...] = jnp.concatenate(rows, 0).astype(jnp.bfloat16)


def join_weight(parts, heads, head_dim):
    _, count, share, _ = parts.shape
    return call(
        functools.partial(weight_kernel, heads, head_dim),
        jax.ShapeDtypeStruct((heads * 3 * head_dim, count * share), jnp.bfloat16),
        (parts,),
        grant=16,
    )


def project_kernel(kv_width, place_ref, weight_ref, mine_ref, other_ref, kv_ref, *q_refs):
    half = mine_ref.shape[0]
    for part, ref in ((place_ref[0], mine_ref), (1 - place_ref[0], other_ref)):
        span = pl.ds(pl.multiple_of(part * half, half), half)
        mixed = dot_nt(weight_ref[...] if q_refs else weight_ref[:kv_width], ref[...]).astype(jnp.bfloat16)
        kv_ref[:, span] = mixed[:kv_width]
        for q_ref in q_refs:
            q_ref[:, span] = mixed[kv_width:]


def project(place, weight, mine, other, kv_width, with_queries=True):
    half, width = mine.shape
    rows = 2 * half
    out_width = weight.shape[0]
    return call(
        functools.partial(project_kernel, kv_width),
        (
            jax.ShapeDtypeStruct((kv_width, rows), jnp.bfloat16),
            jax.ShapeDtypeStruct((out_width - kv_width, rows), jnp.bfloat16),
        )[: 2 if with_queries else 1],
        (place, weight, mine, other),
        flops=2 * rows * width * out_width,
        moved=2 * (rows * width + width * out_width + rows * out_width),
    )


def unpack_queries(ref, frame, heads, head_dim, q_all):
    queries = ref[...].astype(jnp.float32)
    for head in range(heads):
        q_all[frame * heads + head] = queries[head * head_dim : (head + 1) * head_dim].astype(jnp.bfloat16)


def unpack_keyvals(ref, base, side, heads, head_dim, k_all, v_all):
    rows = ref.shape[1]
    ones = jnp.ones((v_all.shape[1] - head_dim, rows), jnp.float32)
    keyvals = ref[...].astype(jnp.float32)
    span = pl.ds(side * rows, rows)
    for head in range(heads):
        keys = keyvals[head * head_dim : (head + 1) * head_dim]
        k_all[base + head, span, :] = keys.T.astype(jnp.bfloat16)
        first = (heads + head) * head_dim
        values = jnp.concatenate([keyvals[first : first + head_dim], ones], 0)
        v_all[base + head, :, span] = values.astype(jnp.bfloat16)


def run_items(items, q_list, k_list, key_rows, heads, head_dim, q_all, k_all, v_all, scores_of, block_high, scale_old, high, total):
    factor = math.log2(math.e) / math.sqrt(head_dim)
    step = math.gcd(key_rows, 256)

    def stage(now, before):
        if now is not None:
            head_a, item_a = now
            state_a = q_list[item_a] * heads + head_a
            key_a = k_list[item_a] * heads + head_a
            queries = q_all[state_a]
            old = high[state_a]
            top = old
        if before is not None:
            head_b, item_b = before
            state_b = q_list[item_b] * heads + head_b
            key_b = k_list[item_b] * heads + head_b
            top_b = block_high[head_b]
            running = total[state_b] * scale_old[head_b]
        for start in range(0, key_rows, step):
            part = pl.ds(start, step)
            if now is not None:
                scores = dot_nn(k_all[key_a, part, :], queries)
                scores_of[head_a][part, :] = scores
                top = jnp.maximum(top, jnp.max(scores, axis=0, keepdims=True))
            if before is not None:
                probs = jnp.exp2((scores_of[head_b][part, :] - top_b) * factor).astype(jnp.bfloat16)
                running = running + dot_nn(v_all[key_b, :, part], probs)
        if before is not None:
            total[state_b] = running
        if now is not None:
            scale_old[head_a] = jnp.exp2((old - top) * factor)
            block_high[head_a] = top
            high[state_a] = top

    def body(index, carry):
        stage((1, index), (0, index))
        stage((0, index + 1), (1, index))
        return carry

    stage((0, 0), None)
    lax.fori_loop(0, items - 1, body, 0)
    stage((1, items - 1), (0, items - 1))
    stage(None, (1, items - 1))


def list_items(count, anchor, keep, q_list, k_list):
    items = jnp.int32(0)
    for frame in range(count):
        pairs = [(jnp.int32(frame), None)]
        if frame > 0:
            pairs.append((jnp.int32(frame - 1), None))
        pairs.append((anchor, (anchor != frame) & (anchor != frame - 1)))
        for key, valid in pairs:
            q_list[items] = frame
            k_list[items] = key
            kept = keep(frame, key)
            items += jnp.where(kept if valid is None else kept & valid, 1, 0)
    return items


def first_kernel(count, heads, head_dim, *refs):
    ids_ref = refs[0]
    q_refs = refs[1 : 1 + count]
    near_refs = refs[1 + count : 1 + 2 * count]
    far_refs = refs[1 + 2 * count : 3 * count]
    high, total = refs[3 * count : 3 * count + 2]
    q_all, k_all, v_all, even, odd, block_high, scale_old, q_list, k_list = refs[3 * count + 2 :]
    rows = q_refs[0].shape[1]
    for slot in range(count):
        frame = ids_ref[slot]
        unpack_queries(q_refs[slot], frame, heads, head_dim, q_all)
        unpack_keyvals(near_refs[slot], frame * heads, 0, heads, head_dim, k_all, v_all)
        if slot < count - 1:
            unpack_keyvals(far_refs[slot], frame * heads, 1, heads, head_dim, k_all, v_all)
    anchor = ids_ref[count]
    late = ids_ref[count - 1]
    high[...] = jnp.full_like(high, -1e30)
    total[...] = jnp.zeros_like(total)
    rest = (heads, head_dim, q_all, k_all, v_all, (even, odd), block_high, scale_old, high, total)
    items = list_items(count, anchor, lambda q, k: k != late, q_list, k_list)
    run_items(items, q_list, k_list, 2 * rows, *rest)
    items = list_items(count, anchor, lambda q, k: k == late, q_list, k_list)
    run_items(items, q_list, k_list, rows, *rest)


def second_kernel(count, heads, head_dim, *refs):
    ids_ref = refs[0]
    q_refs = refs[1 : 1 + count]
    far_ref, high_in, total_in, out_ref = refs[1 + count : 5 + count]
    high, total, q_all, k_late, v_late, even, odd, block_high, scale_old, q_list, k_list = refs[5 + count :]
    rows = q_refs[0].shape[1]
    for slot in range(count):
        unpack_queries(q_refs[slot], ids_ref[slot], heads, head_dim, q_all)
    unpack_keyvals(far_ref, 0, 0, heads, head_dim, k_late, v_late)
    high[...] = high_in[...]
    total[...] = total_in[...]
    late = ids_ref[count - 1]
    items = list_items(count, ids_ref[count], lambda q, k: k == late, q_list, k_list)
    for item in range(count):
        k_list[item] = 0
    run_items(
        items, q_list, k_list, rows, heads, head_dim, q_all, k_late, v_late, (even, odd), block_high, scale_old, high, total
    )
    for frame in range(count):
        parts = []
        for head in range(heads):
            sums = total[frame * heads + head]
            parts.append(sums[:head_dim] / sums[head_dim : head_dim + 1])
        out_ref[frame] = jnp.concatenate(parts, 0).astype(jnp.bfloat16)


def attend_all(ids, queries, near, far, heads, head_dim):
    count = len(queries)
    rows = queries[0].shape[1]
    value_rows = head_dim + 8
    states = count * heads
    f32 = jnp.float32
    lists = [pltpu.SMEM((3 * count + 1,), jnp.int32)] * 2
    tops = [pltpu.VMEM((heads, 1, rows), f32)] * 2
    state = (
        jax.ShapeDtypeStruct((states, 1, rows), f32),
        jax.ShapeDtypeStruct((states, value_rows, rows), f32),
    )
    high, total = call(
        functools.partial(first_kernel, count, heads, head_dim),
        state,
        (ids, *queries, *near, *far[:-1]),
        [
            pltpu.VMEM((states, head_dim, rows), jnp.bfloat16),
            pltpu.VMEM((states, 2 * rows, head_dim), jnp.bfloat16),
            pltpu.VMEM((states, value_rows, 2 * rows), jnp.bfloat16),
            pltpu.VMEM((2 * rows, rows), f32),
            pltpu.VMEM((2 * rows, rows), f32),
            *tops,
            *lists,
        ],
        flops=3 * count * heads * rows * 2 * rows * head_dim * 16,
        moved=2 * count * heads * head_dim * rows * 6,
        grant=24,
    )
    return call(
        functools.partial(second_kernel, count, heads, head_dim),
        jax.ShapeDtypeStruct((count, heads * head_dim, rows), jnp.bfloat16),
        (ids, *queries, far[-1], high, total),
        [
            pltpu.VMEM(state[0].shape, f32),
            pltpu.VMEM(state[1].shape, f32),
            pltpu.VMEM((states, head_dim, rows), jnp.bfloat16),
            pltpu.VMEM((heads, rows, head_dim), jnp.bfloat16),
            pltpu.VMEM((heads, value_rows, rows), jnp.bfloat16),
            pltpu.VMEM((rows, rows), f32),
            pltpu.VMEM((rows, rows), f32),
            *tops,
            *lists,
        ],
        flops=heads * rows * rows * head_dim * 16,
        moved=2 * count * heads * head_dim * rows * 6,
        grant=16,
    )


def residual_kernel(core_ref, frame_ref, mod_ref, out_ref, gate_ref):
    width = out_ref.shape[0]
    frame = frame_ref[...].astype(jnp.float32)
    mine = jnp.where(core_ref[0] == 0, frame[:, :width], frame[:, width:])
    out_ref[...] = mine.T.astype(jnp.bfloat16)
    gate = jnp.broadcast_to(mod_ref[2:3, :], (8, 2 * width))
    gate = jnp.where(core_ref[0] == 0, gate[:, :width], gate[:, width:])
    gate_ref[...] = gate.T


def residual(core, frame, modulation):
    rows, width = frame.shape
    return call(
        residual_kernel,
        (jax.ShapeDtypeStruct((width // 2, rows), jnp.bfloat16), jax.ShapeDtypeStruct((width // 2, 8), jnp.float32)),
        (core, frame, modulation),
        flops=4 * rows * width,
        moved=3 * rows * width,
        grant=16,
    )


def order_kernel(where_ref, mine_ref, other_ref, near_ref, send_ref):
    group, core = where_ref[1], where_ref[3]
    block = mine_ref.shape[1]
    per_core = mine_ref.shape[0] // 2
    for same, ref in ((True, mine_ref), (False, other_ref)):
        half = group if same else 1 - group
        for index in range(per_core):
            start = pl.multiple_of((index * 2 + half) * block, block)
            near_ref[pl.ds(start, block), :] = ref[core * per_core + index]
            send_ref[pl.ds(start, block), :] = ref[(1 - core) * per_core + index]


def order_columns(where, mine, other):
    count, block, depth = mine.shape
    out = jax.ShapeDtypeStruct((count * block, depth), mine.dtype)
    return call(order_kernel, (out, out), (where, mine, other), moved=8 * mine.size, grant=8)


def near_kernel(weight_ref, near_ref, frame_ref, gate_ref, out_ref):
    projected = dot_nn(weight_ref[...], near_ref[...])
    out_ref[...] = frame_ref[...].astype(jnp.float32) + gate_ref[:, 0:1] * projected


def far_kernel(weight_ref, far_ref, near_sum_ref, gate_ref, out_ref):
    projected = dot_nn(weight_ref[...], far_ref[...])
    out_ref[...] = (near_sum_ref[...] + gate_ref[:, 0:1] * projected).astype(jnp.bfloat16)


def finish_near(weight, near, frame_part, gate_part):
    out = jax.ShapeDtypeStruct(frame_part.shape, jnp.float32)
    return call(near_kernel, out, (weight, near, frame_part, gate_part), grant=16)


def finish_far(weight, far, near_sum, gate_part):
    out = jax.ShapeDtypeStruct(near_sum.shape, jnp.bfloat16)
    return call(far_kernel, out, (weight, far, near_sum, gate_part), grant=16)


def swapped(block, axis):
    return lax.ppermute(block, axis, [(0, 1), (1, 0)])


def shifted(block, axis, distance):
    devices = range(lax.axis_size(axis))
    route = [(i - distance, i) for i in devices if i - distance in devices]
    return lax.ppermute(block, axis, route)


def from_partner(block, axis, stride):
    count = lax.axis_size(axis)
    route = []
    for low in range(count):
        high = low | 1 << stride
        if high != low and high < count:
            route += [(low, high), (high, low)]
    return lax.ppermute(block, axis, route)


def attend(queries, kv_all, first_frame, anchor, head_dim):
    frame_count, query_rows, query_width = queries.shape
    key_count = kv_all.shape[1]
    head_count = query_width // head_dim
    block_rows = math.gcd(512, query_rows)
    kv_heads = kv_all.reshape(frame_count + 2, key_count, head_count, 2, head_dim)
    global_idx = first_frame + 0
    use_prev = global_idx > 0
    use_anchor = (anchor != global_idx) & (anchor != global_idx - 1)
    valid_keys = jnp.concatenate(
        [
            jnp.broadcast_to(use_anchor, (key_count,)),
            jnp.broadcast_to(use_prev, (key_count,)),
            jnp.ones((key_count,), bool),
        ]
    )
    frame_queries = queries[0]

    def one_head(head_idx):
        picked = lax.dynamic_index_in_dim(kv_heads, head_idx, 2, keepdims=False)
        key_rows = jnp.concatenate(
            [picked[frame_count + 1, :, 0], picked[frame_count, :, 0], picked[0, :, 0]], 0
        )
        val_rows = jnp.concatenate(
            [picked[frame_count + 1, :, 1], picked[frame_count, :, 1], picked[0, :, 1]], 0
        )
        query_head = lax.dynamic_slice_in_dim(frame_queries, head_idx * head_dim, head_dim, 1)
        query_blocks = query_head.reshape(query_rows // block_rows, block_rows, head_dim)

        def one_block(query_block):
            scores = lax.dot_general(
                query_block, key_rows, (((1,), (1,)), ((), ())), preferred_element_type=jnp.float32
            ) * head_dim ** (-0.5)
            scores = jnp.where(valid_keys[None, :], scores, -1e30)
            row_max = jnp.max(scores, axis=-1, keepdims=True)
            probs = jnp.exp(scores - row_max)
            denominator = jnp.sum(probs, axis=-1, keepdims=True)
            numerator = jnp.dot(
                probs.astype(jnp.bfloat16), val_rows, preferred_element_type=jnp.float32
            )
            return (numerator / denominator).astype(jnp.bfloat16)

        return lax.map(one_block, query_blocks).reshape(query_rows, head_dim)

    per_head = lax.map(one_head, jnp.arange(head_count, dtype=jnp.int32))
    frame_outputs = [jnp.transpose(per_head, (1, 0, 2)).reshape(query_rows, head_count * head_dim)]
    return jnp.stack(frame_outputs)


def by_frames(frames, modulation, w_qkv, w_out, anchor_offsets):
    frame_count, row_count, model_width = frames.shape
    head_local = w_qkv.shape[1]
    head_dim = w_qkv.shape[3]
    my_index = lax.axis_index("frame")
    flat_rows = frames.reshape(frame_count * row_count, model_width).astype(jnp.float32)
    row_mean = jnp.mean(flat_rows, axis=-1, keepdims=True)
    centred = flat_rows - row_mean
    row_var = jnp.mean(centred * centred, axis=-1, keepdims=True)
    normed = centred * lax.rsqrt(row_var + 1e-06)
    hidden = (normed * (1.0 + modulation[1]) + modulation[0]).astype(jnp.bfloat16)
    full_weight = lax.all_gather(w_qkv, "frame", axis=0, tiled=True)
    mixed = jnp.dot(
        hidden,
        full_weight.reshape(model_width, head_local * 3 * head_dim),
        preferred_element_type=jnp.float32,
    )
    mixed = mixed.astype(jnp.bfloat16).reshape(frame_count, row_count, head_local, 3, head_dim)
    queries = mixed[:, :, :, 0, :].reshape(frame_count, row_count, head_local * head_dim)
    keyvals = mixed[:, :, :, 1:, :].reshape(frame_count, row_count, head_local * 2 * head_dim)
    span_count = anchor_offsets.shape[0]
    total_frames = frame_count * lax.axis_size("frame")
    span_len = total_frames // span_count
    first_frame = my_index * frame_count
    mine_span = first_frame // span_len
    anchor = mine_span * span_len + anchor_offsets[mine_span]
    prev_kv = shifted(keyvals[frame_count - 1], "frame", 1)
    holder = anchor // frame_count
    anchor_kv = lax.dynamic_index_in_dim(keyvals, anchor % frame_count, 0, keepdims=False)
    levels = (span_len // frame_count).bit_length() - 1
    for bit_index in range(levels):
        partner = from_partner(anchor_kv, "frame", bit_index)
        take_partner = my_index >> bit_index & 1 != holder >> bit_index & 1
        anchor_kv = jnp.where(take_partner, partner, anchor_kv)
    kv_all = jnp.concatenate([keyvals, prev_kv[None], anchor_kv[None]], 0)
    kv_whole = lax.all_gather(kv_all, "tok", axis=1, tiled=True)
    attended = attend(queries, kv_whole, first_frame, anchor, head_dim)
    flat_attended = attended.reshape(frame_count * row_count, head_local * head_dim)
    term_cols = jnp.dot(
        flat_attended,
        lax.all_gather(w_out, "frame", axis=1, tiled=True),
        preferred_element_type=jnp.float32,
    )
    summed = lax.psum_scatter(term_cols, "head", scatter_dimension=1, tiled=True)
    half_width = summed.shape[1]
    col_start = lax.axis_index("head") * half_width
    residual_in = lax.dynamic_slice_in_dim(flat_rows, col_start, half_width, 1)
    gate_part = lax.dynamic_slice_in_dim(modulation[2], col_start, half_width, 0)
    result = (residual_in + gate_part * summed).astype(jnp.bfloat16)
    return result.reshape(frame_count, row_count, half_width)


def flipped(block, axis, distance):
    return lax.ppermute(block, axis, [(i, i ^ distance) for i in range(lax.axis_size(axis))])


def after(block, other):
    return lax.optimization_barrier((block, other))[0]


def by_heads(frames, modulation, w_qkv, w_out, anchor_offsets):
    _, rows, width = frames.shape
    share, head_local, _, head_dim = w_qkv.shape
    count = lax.axis_size("frame")
    heads = head_local // count
    core = lax.axis_index("head")
    me = lax.axis_index("frame")
    group = lax.axis_index("groups")
    frame = frames[0]
    place = core.reshape(1).astype(jnp.int32)

    tok = lax.axis_index("tok")
    where = jnp.stack([me, group, tok, core]).astype(jnp.int32)

    blocks = jnp.transpose(w_qkv, (1, 2, 3, 0)).reshape(count, heads, 3 * head_dim, share)
    part_rows = -(-3 * head_dim // 32) * 16
    start = tok * (3 * head_dim - part_rows)
    part = lax.dynamic_slice(blocks, (0, group, start, 0), (count, 1, part_rows, share))[:, 0]
    part = jnp.transpose(part, (0, 2, 1))
    part = lax.all_to_all(part, "frame", 0, 0)
    plane = lax.all_to_all(jnp.broadcast_to(part[None], (4, *part.shape)), ("groups", "tok"), 0, 0)
    weight = join_weight(plane, heads, head_dim)
    kv_width = 2 * heads * head_dim

    mine = norm_half(place, frame, modulation)
    arrivals = [mine, flipped(mine, "frame", 1), flipped(mine, "frame", 2)]
    arrivals.append(flipped(arrivals[2], "frame", 1))
    frame_part, gate_part = residual(place, after(frame, arrivals[1]), modulation)

    queries, near, far = [], [], []
    for distance, block in enumerate(arrivals):
        if distance == 3:
            block = after(block, (frame_part, near[0], near[1], near[2]))
        kv, q = project(place, weight, block, swapped(block, "head"), kv_width)
        queries.append(q)
        near.append(kv)
        if distance == 0:
            across = swapped(block, "tok")
            far += project(place, weight, across, swapped(across, "head"), kv_width, False)
        else:
            far.append(swapped(kv, "tok"))
    ids = jnp.stack([me ^ distance for distance in range(count)] + [anchor_offsets[0]]).astype(jnp.int32)
    attended = attend_all(ids, queries, near, far, heads, head_dim)
    arrived = lax.all_to_all(attended, "frame", 0, 0).reshape(count * heads * head_dim, rows)
    arrived_far = swapped(arrived, "head")

    columns = w_out.shape[1] // 2
    w_part = lax.dynamic_slice_in_dim(w_out.T, group * columns, columns, 0)
    w_part = after(w_part, near[-1])
    w_part = lax.all_to_all(jnp.broadcast_to(w_part[None], (count, *w_part.shape)), "frame", 0, 0)
    near_w, send_w = order_columns(where, w_part, swapped(w_part, "groups"))
    far_w = swapped(send_w, "head")
    near_sum = finish_near(near_w, arrived, frame_part, gate_part)
    updated = finish_far(far_w, arrived_far, near_sum, gate_part)
    return updated.T[None]


def on_device(frames, modulation, w_qkv, w_out, anchor_offsets):
    count = lax.axis_size("frame")
    fits = (
        frames.shape[0] == 1
        and anchor_offsets.shape[0] == 1
        and count == 4
        and lax.axis_size("groups") == 2
        and lax.axis_size("head") == 2
        and lax.axis_size("tok") == 2
        and w_qkv.shape[1] == 2 * count
        and w_qkv.shape[3] % 8 == 0
        and frames.shape[1] % 256 == 0
        and frames.shape[2] % 32 == 0
    )
    step = by_heads if fits else by_frames
    return step(frames, modulation, w_qkv, w_out, anchor_offsets)


def solution(mesh):
    placed = (
        P(("groups", "frame"), "tok", None),
        P(),
        P("frame", "head", None, None),
        P("head", "frame"),
        P("groups"),
    )
    return jax.shard_map(
        on_device,
        mesh=mesh,
        in_specs=placed,
        out_specs=P(("groups", "frame"), "tok", "head"),
        check_vma=False,
    )
```

```python
import functools
import math

import jax
import jax.numpy as jnp
from jax import lax
from jax.experimental import pallas as pl
from jax.experimental.pallas import tpu as pltpu
from jax.sharding import PartitionSpec as P

MIB = 2**20


def dot_nn(a, b):
    return lax.dot_general(a, b, (((1,), (0,)), ((), ())), preferred_element_type=jnp.float32)


def dot_nt(a, b):
    return lax.dot_general(a, b, (((1,), (1,)), ((), ())), preferred_element_type=jnp.float32)


def call(kernel, out_shape, operands, scratch=(), flops=0, moved=0, left=(), grant=8):
    smem = pl.BlockSpec(memory_space=pltpu.SMEM)
    vmem = pl.BlockSpec(memory_space=pltpu.VMEM)
    where = pl.BlockSpec(memory_space=pl.ANY)
    many = isinstance(out_shape, (list, tuple))
    return pl.pallas_call(
        kernel,
        out_shape=out_shape,
        in_specs=[where if i in left else smem if x.dtype == jnp.int32 else vmem for i, x in enumerate(operands)],
        out_specs=[vmem] * len(out_shape) if many else vmem,
        scratch_shapes=list(scratch),
        compiler_params=pltpu.CompilerParams(vmem_limit_bytes=grant * MIB),
        cost_estimate=pl.CostEstimate(flops=flops, bytes_accessed=moved, transcendentals=0),
    )(*operands)


def norm_kernel(place_ref, frame_ref, mod_ref, out_ref, rows, arrived):
    half = out_ref.shape[0]
    start = pl.multiple_of(place_ref[0] * half, half)
    copy = pltpu.make_async_copy(frame_ref.at[pl.ds(start, half), :], rows, arrived)
    copy.start()
    copy.wait()
    values = rows[...].astype(jnp.float32)
    row_mean = jnp.mean(values, axis=-1, keepdims=True)
    centred = values - row_mean
    row_var = jnp.mean(centred * centred, axis=-1, keepdims=True)
    normed = centred * lax.rsqrt(row_var + 1e-06)
    out_ref[...] = (normed * (1.0 + mod_ref[1:2, :]) + mod_ref[0:1, :]).astype(jnp.bfloat16)


def norm_half(place, frame, modulation):
    half, width = frame.shape[0] // 2, frame.shape[1]
    return call(
        norm_kernel,
        jax.ShapeDtypeStruct((half, width), jnp.bfloat16),
        (place, frame, modulation),
        [pltpu.VMEM((half, width), jnp.bfloat16), pltpu.SemaphoreType.DMA],
        flops=20 * half * width,
        moved=4 * half * width,
        left=(1,),
    )


def weight_kernel(heads, head_dim, parts_ref, out_ref):
    _, count, share, part_rows = parts_ref.shape
    head_rows = 3 * head_dim
    per_head = []
    for head in range(heads):
        low, high = [
            jnp.concatenate([parts_ref[head * 2 + i, source] for source in range(count)], 0).astype(jnp.float32).T
            for i in range(2)
        ]
        per_head.append(jnp.concatenate([low, high[2 * part_rows - head_rows :]], 0))
    rows = [w[kind * head_dim : (kind + 1) * head_dim] for kind in (1, 2, 0) for w in per_head]
    out_ref[...] = jnp.concatenate(rows, 0).astype(jnp.bfloat16)


def join_weight(parts, heads, head_dim):
    _, count, share, _ = parts.shape
    return call(
        functools.partial(weight_kernel, heads, head_dim),
        jax.ShapeDtypeStruct((heads * 3 * head_dim, count * share), jnp.bfloat16),
        (parts,),
        grant=16,
    )


def project_kernel(kv_width, place_ref, weight_ref, mine_ref, other_ref, kv_ref, *q_refs):
    half = mine_ref.shape[0]
    for part, ref in ((place_ref[0], mine_ref), (1 - place_ref[0], other_ref)):
        span = pl.ds(pl.multiple_of(part * half, half), half)
        mixed = dot_nt(weight_ref[...] if q_refs else weight_ref[:kv_width], ref[...]).astype(jnp.bfloat16)
        kv_ref[:, span] = mixed[:kv_width]
        for q_ref in q_refs:
            q_ref[:, span] = mixed[kv_width:]


def project(place, weight, mine, other, kv_width, with_queries=True):
    half, width = mine.shape
    rows = 2 * half
    out_width = weight.shape[0]
    return call(
        functools.partial(project_kernel, kv_width),
        (
            jax.ShapeDtypeStruct((kv_width, rows), jnp.bfloat16),
            jax.ShapeDtypeStruct((out_width - kv_width, rows), jnp.bfloat16),
        )[: 2 if with_queries else 1],
        (place, weight, mine, other),
        flops=2 * rows * width * out_width,
        moved=2 * (rows * width + width * out_width + rows * out_width),
    )


def unpack_queries(ref, frame, heads, head_dim, q_all):
    queries = ref[...].astype(jnp.float32)
    for head in range(heads):
        q_all[frame * heads + head] = queries[head * head_dim : (head + 1) * head_dim].astype(jnp.bfloat16)


def unpack_keyvals(ref, base, side, heads, head_dim, k_all, v_all):
    rows = ref.shape[1]
    ones = jnp.ones((v_all.shape[1] - head_dim, rows), jnp.float32)
    keyvals = ref[...].astype(jnp.float32)
    span = pl.ds(side * rows, rows)
    for head in range(heads):
        keys = keyvals[head * head_dim : (head + 1) * head_dim]
        k_all[base + head, span, :] = keys.T.astype(jnp.bfloat16)
        first = (heads + head) * head_dim
        values = jnp.concatenate([keyvals[first : first + head_dim], ones], 0)
        v_all[base + head, :, span] = values.astype(jnp.bfloat16)


def run_items(items, q_list, k_list, key_rows, heads, head_dim, q_all, k_all, v_all, scores_of, block_high, scale_old, high, total):
    factor = math.log2(math.e) / math.sqrt(head_dim)
    step = math.gcd(key_rows, 256)

    def stage(now, before):
        if now is not None:
            head_a, item_a = now
            state_a = q_list[item_a] * heads + head_a
            key_a = k_list[item_a] * heads + head_a
            queries = q_all[state_a]
            old = high[state_a]
            top = old
        if before is not None:
            head_b, item_b = before
            state_b = q_list[item_b] * heads + head_b
            key_b = k_list[item_b] * heads + head_b
            top_b = block_high[head_b]
            running = total[state_b] * scale_old[head_b]
        for start in range(0, key_rows, step):
            part = pl.ds(start, step)
            if now is not None:
                scores = dot_nn(k_all[key_a, part, :], queries)
                scores_of[head_a][part, :] = scores
                top = jnp.maximum(top, jnp.max(scores, axis=0, keepdims=True))
            if before is not None:
                probs = jnp.exp2((scores_of[head_b][part, :] - top_b) * factor).astype(jnp.bfloat16)
                running = running + dot_nn(v_all[key_b, :, part], probs)
        if before is not None:
            total[state_b] = running
        if now is not None:
            scale_old[head_a] = jnp.exp2((old - top) * factor)
            block_high[head_a] = top
            high[state_a] = top

    def body(index, carry):
        stage((1, index), (0, index))
        stage((0, index + 1), (1, index))
        return carry

    stage((0, 0), None)
    lax.fori_loop(0, items - 1, body, 0)
    stage((1, items - 1), (0, items - 1))
    stage(None, (1, items - 1))


def list_items(count, anchor, keep, q_list, k_list):
    items = jnp.int32(0)
    for frame in range(count):
        pairs = [(jnp.int32(frame), None)]
        if frame > 0:
            pairs.append((jnp.int32(frame - 1), None))
        pairs.append((anchor, (anchor != frame) & (anchor != frame - 1)))
        for key, valid in pairs:
            q_list[items] = frame
            k_list[items] = key
            kept = keep(frame, key)
            items += jnp.where(kept if valid is None else kept & valid, 1, 0)
    return items


def first_kernel(count, heads, head_dim, *refs):
    ids_ref = refs[0]
    q_refs = refs[1 : 1 + count]
    near_refs = refs[1 + count : 1 + 2 * count]
    far_refs = refs[1 + 2 * count : 3 * count]
    high, total = refs[3 * count : 3 * count + 2]
    q_all, k_all, v_all, even, odd, block_high, scale_old, q_list, k_list = refs[3 * count + 2 :]
    rows = q_refs[0].shape[1]
    for slot in range(count):
        frame = ids_ref[slot]
        unpack_queries(q_refs[slot], frame, heads, head_dim, q_all)
        unpack_keyvals(near_refs[slot], frame * heads, 0, heads, head_dim, k_all, v_all)
        if slot < count - 1:
            unpack_keyvals(far_refs[slot], frame * heads, 1, heads, head_dim, k_all, v_all)
    anchor = ids_ref[count]
    late = ids_ref[count - 1]
    high[...] = jnp.full_like(high, -1e30)
    total[...] = jnp.zeros_like(total)
    rest = (heads, head_dim, q_all, k_all, v_all, (even, odd), block_high, scale_old, high, total)
    items = list_items(count, anchor, lambda q, k: k != late, q_list, k_list)
    run_items(items, q_list, k_list, 2 * rows, *rest)
    items = list_items(count, anchor, lambda q, k: k == late, q_list, k_list)
    run_items(items, q_list, k_list, rows, *rest)


def second_kernel(count, heads, head_dim, *refs):
    ids_ref = refs[0]
    q_refs = refs[1 : 1 + count]
    far_ref, high_in, total_in, out_ref = refs[1 + count : 5 + count]
    high, total, q_all, k_late, v_late, even, odd, block_high, scale_old, q_list, k_list = refs[5 + count :]
    rows = q_refs[0].shape[1]
    for slot in range(count):
        unpack_queries(q_refs[slot], ids_ref[slot], heads, head_dim, q_all)
    unpack_keyvals(far_ref, 0, 0, heads, head_dim, k_late, v_late)
    high[...] = high_in[...]
    total[...] = total_in[...]
    late = ids_ref[count - 1]
    items = list_items(count, ids_ref[count], lambda q, k: k == late, q_list, k_list)
    for item in range(count):
        k_list[item] = 0
    run_items(
        items, q_list, k_list, rows, heads, head_dim, q_all, k_late, v_late, (even, odd), block_high, scale_old, high, total
    )
    for frame in range(count):
        parts = []
        for head in range(heads):
            sums = total[frame * heads + head]
            parts.append(sums[:head_dim] / sums[head_dim : head_dim + 1])
        out_ref[frame] = jnp.concatenate(parts, 0).astype(jnp.bfloat16)


def attend_all(ids, queries, near, far, heads, head_dim):
    count = len(queries)
    rows = queries[0].shape[1]
    value_rows = head_dim + 8
    states = count * heads
    f32 = jnp.float32
    lists = [pltpu.SMEM((3 * count + 1,), jnp.int32)] * 2
    tops = [pltpu.VMEM((heads, 1, rows), f32)] * 2
    state = (
        jax.ShapeDtypeStruct((states, 1, rows), f32),
        jax.ShapeDtypeStruct((states, value_rows, rows), f32),
    )
    high, total = call(
        functools.partial(first_kernel, count, heads, head_dim),
        state,
        (ids, *queries, *near, *far[:-1]),
        [
            pltpu.VMEM((states, head_dim, rows), jnp.bfloat16),
            pltpu.VMEM((states, 2 * rows, head_dim), jnp.bfloat16),
            pltpu.VMEM((states, value_rows, 2 * rows), jnp.bfloat16),
            pltpu.VMEM((2 * rows, rows), f32),
            pltpu.VMEM((2 * rows, rows), f32),
            *tops,
            *lists,
        ],
        flops=3 * count * heads * rows * 2 * rows * head_dim * 16,
        moved=2 * count * heads * head_dim * rows * 6,
        grant=24,
    )
    return call(
        functools.partial(second_kernel, count, heads, head_dim),
        jax.ShapeDtypeStruct((count, heads * head_dim, rows), jnp.bfloat16),
        (ids, *queries, far[-1], high, total),
        [
            pltpu.VMEM(state[0].shape, f32),
            pltpu.VMEM(state[1].shape, f32),
            pltpu.VMEM((states, head_dim, rows), jnp.bfloat16),
            pltpu.VMEM((heads, rows, head_dim), jnp.bfloat16),
            pltpu.VMEM((heads, value_rows, rows), jnp.bfloat16),
            pltpu.VMEM((rows, rows), f32),
            pltpu.VMEM((rows, rows), f32),
            *tops,
            *lists,
        ],
        flops=heads * rows * rows * head_dim * 16,
        moved=2 * count * heads * head_dim * rows * 6,
        grant=16,
    )


def residual_kernel(core_ref, frame_ref, mod_ref, out_ref, gate_ref):
    width = out_ref.shape[0]
    frame = frame_ref[...].astype(jnp.float32)
    mine = jnp.where(core_ref[0] == 0, frame[:, :width], frame[:, width:])
    out_ref[...] = mine.T.astype(jnp.bfloat16)
    gate = jnp.broadcast_to(mod_ref[2:3, :], (8, 2 * width))
    gate = jnp.where(core_ref[0] == 0, gate[:, :width], gate[:, width:])
    gate_ref[...] = gate.T


def residual(core, frame, modulation):
    rows, width = frame.shape
    return call(
        residual_kernel,
        (jax.ShapeDtypeStruct((width // 2, rows), jnp.bfloat16), jax.ShapeDtypeStruct((width // 2, 8), jnp.float32)),
        (core, frame, modulation),
        flops=4 * rows * width,
        moved=3 * rows * width,
        grant=16,
    )


def part_kernel(where_ref, mine_ref, other_ref, heads_ref, start_ref, gate_ref, out_ref, weight):
    group, core = where_ref[1], where_ref[3]
    block = mine_ref.shape[1]
    per_core = mine_ref.shape[0] // 2
    for same, ref in ((True, mine_ref), (False, other_ref)):
        half = group if same else 1 - group
        for index in range(per_core):
            start = pl.multiple_of((index * 2 + half) * block, block)
            weight[pl.ds(start, block), :] = ref[core * per_core + index]
    projected = dot_nn(weight[...], heads_ref[...])
    out_ref[...] = (start_ref[...].astype(jnp.float32) + gate_ref[:, 0:1] * projected).astype(out_ref.dtype)


def add_part(where, mine, other, heads, start, gate, dtype):
    return call(
        part_kernel,
        jax.ShapeDtypeStruct(start.shape, dtype),
        (where, mine, other, heads, start, gate),
        [pltpu.VMEM((start.shape[0], mine.shape[2]), jnp.bfloat16)],
        grant=16,
    )


def swapped(block, axis):
    return lax.ppermute(block, axis, [(0, 1), (1, 0)])


def shifted(block, axis, distance):
    devices = range(lax.axis_size(axis))
    route = [(i - distance, i) for i in devices if i - distance in devices]
    return lax.ppermute(block, axis, route)


def from_partner(block, axis, stride):
    count = lax.axis_size(axis)
    route = []
    for low in range(count):
        high = low | 1 << stride
        if high != low and high < count:
            route += [(low, high), (high, low)]
    return lax.ppermute(block, axis, route)


def attend(queries, kv_all, first_frame, anchor, head_dim):
    frame_count, query_rows, query_width = queries.shape
    key_count = kv_all.shape[1]
    head_count = query_width // head_dim
    block_rows = math.gcd(512, query_rows)
    kv_heads = kv_all.reshape(frame_count + 2, key_count, head_count, 2, head_dim)
    global_idx = first_frame + 0
    use_prev = global_idx > 0
    use_anchor = (anchor != global_idx) & (anchor != global_idx - 1)
    valid_keys = jnp.concatenate(
        [
            jnp.broadcast_to(use_anchor, (key_count,)),
            jnp.broadcast_to(use_prev, (key_count,)),
            jnp.ones((key_count,), bool),
        ]
    )
    frame_queries = queries[0]

    def one_head(head_idx):
        picked = lax.dynamic_index_in_dim(kv_heads, head_idx, 2, keepdims=False)
        key_rows = jnp.concatenate(
            [picked[frame_count + 1, :, 0], picked[frame_count, :, 0], picked[0, :, 0]], 0
        )
        val_rows = jnp.concatenate(
            [picked[frame_count + 1, :, 1], picked[frame_count, :, 1], picked[0, :, 1]], 0
        )
        query_head = lax.dynamic_slice_in_dim(frame_queries, head_idx * head_dim, head_dim, 1)
        query_blocks = query_head.reshape(query_rows // block_rows, block_rows, head_dim)

        def one_block(query_block):
            scores = lax.dot_general(
                query_block, key_rows, (((1,), (1,)), ((), ())), preferred_element_type=jnp.float32
            ) * head_dim ** (-0.5)
            scores = jnp.where(valid_keys[None, :], scores, -1e30)
            row_max = jnp.max(scores, axis=-1, keepdims=True)
            probs = jnp.exp(scores - row_max)
            denominator = jnp.sum(probs, axis=-1, keepdims=True)
            numerator = jnp.dot(
                probs.astype(jnp.bfloat16), val_rows, preferred_element_type=jnp.float32
            )
            return (numerator / denominator).astype(jnp.bfloat16)

        return lax.map(one_block, query_blocks).reshape(query_rows, head_dim)

    per_head = lax.map(one_head, jnp.arange(head_count, dtype=jnp.int32))
    frame_outputs = [jnp.transpose(per_head, (1, 0, 2)).reshape(query_rows, head_count * head_dim)]
    return jnp.stack(frame_outputs)


def by_frames(frames, modulation, w_qkv, w_out, anchor_offsets):
    frame_count, row_count, model_width = frames.shape
    head_local = w_qkv.shape[1]
    head_dim = w_qkv.shape[3]
    my_index = lax.axis_index("frame")
    flat_rows = frames.reshape(frame_count * row_count, model_width).astype(jnp.float32)
    row_mean = jnp.mean(flat_rows, axis=-1, keepdims=True)
    centred = flat_rows - row_mean
    row_var = jnp.mean(centred * centred, axis=-1, keepdims=True)
    normed = centred * lax.rsqrt(row_var + 1e-06)
    hidden = (normed * (1.0 + modulation[1]) + modulation[0]).astype(jnp.bfloat16)
    full_weight = lax.all_gather(w_qkv, "frame", axis=0, tiled=True)
    mixed = jnp.dot(
        hidden,
        full_weight.reshape(model_width, head_local * 3 * head_dim),
        preferred_element_type=jnp.float32,
    )
    mixed = mixed.astype(jnp.bfloat16).reshape(frame_count, row_count, head_local, 3, head_dim)
    queries = mixed[:, :, :, 0, :].reshape(frame_count, row_count, head_local * head_dim)
    keyvals = mixed[:, :, :, 1:, :].reshape(frame_count, row_count, head_local * 2 * head_dim)
    span_count = anchor_offsets.shape[0]
    total_frames = frame_count * lax.axis_size("frame")
    span_len = total_frames // span_count
    first_frame = my_index * frame_count
    mine_span = first_frame // span_len
    anchor = mine_span * span_len + anchor_offsets[mine_span]
    prev_kv = shifted(keyvals[frame_count - 1], "frame", 1)
    holder = anchor // frame_count
    anchor_kv = lax.dynamic_index_in_dim(keyvals, anchor % frame_count, 0, keepdims=False)
    levels = (span_len // frame_count).bit_length() - 1
    for bit_index in range(levels):
        partner = from_partner(anchor_kv, "frame", bit_index)
        take_partner = my_index >> bit_index & 1 != holder >> bit_index & 1
        anchor_kv = jnp.where(take_partner, partner, anchor_kv)
    kv_all = jnp.concatenate([keyvals, prev_kv[None], anchor_kv[None]], 0)
    kv_whole = lax.all_gather(kv_all, "tok", axis=1, tiled=True)
    attended = attend(queries, kv_whole, first_frame, anchor, head_dim)
    flat_attended = attended.reshape(frame_count * row_count, head_local * head_dim)
    term_cols = jnp.dot(
        flat_attended,
        lax.all_gather(w_out, "frame", axis=1, tiled=True),
        preferred_element_type=jnp.float32,
    )
    summed = lax.psum_scatter(term_cols, "head", scatter_dimension=1, tiled=True)
    half_width = summed.shape[1]
    col_start = lax.axis_index("head") * half_width
    residual_in = lax.dynamic_slice_in_dim(flat_rows, col_start, half_width, 1)
    gate_part = lax.dynamic_slice_in_dim(modulation[2], col_start, half_width, 0)
    result = (residual_in + gate_part * summed).astype(jnp.bfloat16)
    return result.reshape(frame_count, row_count, half_width)


def flipped(block, axis, distance):
    return lax.ppermute(block, axis, [(i, i ^ distance) for i in range(lax.axis_size(axis))])


def after(block, other):
    return lax.optimization_barrier((block, other))[0]


def by_heads(frames, modulation, w_qkv, w_out, anchor_offsets):
    _, rows, width = frames.shape
    share, head_local, _, head_dim = w_qkv.shape
    count = lax.axis_size("frame")
    heads = head_local // count
    core = lax.axis_index("head")
    me = lax.axis_index("frame")
    group = lax.axis_index("groups")
    frame = frames[0]
    place = core.reshape(1).astype(jnp.int32)

    tok = lax.axis_index("tok")
    where = jnp.stack([me, group, tok, core]).astype(jnp.int32)

    blocks = jnp.transpose(w_qkv, (1, 2, 3, 0)).reshape(count, heads, 3 * head_dim, share)
    part_rows = -(-3 * head_dim // 32) * 16
    start = tok * (3 * head_dim - part_rows)
    part = lax.dynamic_slice(blocks, (0, group, start, 0), (count, 1, part_rows, share))[:, 0]
    part = jnp.transpose(part, (0, 2, 1))
    part = lax.all_to_all(part, "frame", 0, 0)
    plane = lax.all_to_all(jnp.broadcast_to(part[None], (4, *part.shape)), ("groups", "tok"), 0, 0)
    weight = join_weight(plane, heads, head_dim)
    kv_width = 2 * heads * head_dim

    mine = norm_half(place, frame, modulation)
    arrivals = [mine, flipped(mine, "frame", 1), flipped(mine, "frame", 2)]
    arrivals.append(flipped(arrivals[2], "frame", 1))
    frame_part, gate_part = residual(place, after(frame, arrivals[1]), modulation)

    queries, near, far = [], [], []
    for distance, block in enumerate(arrivals):
        if distance == 3:
            block = after(block, (frame_part, near[0], near[1], near[2]))
        kv, q = project(place, weight, block, swapped(block, "head"), kv_width)
        queries.append(q)
        near.append(kv)
        if distance == 0:
            across = after(swapped(block, "tok"), kv)
            far += project(place, weight, across, swapped(across, "head"), kv_width, False)
        else:
            far.append(swapped(kv, "tok"))
    ids = jnp.stack([me ^ distance for distance in range(count)] + [anchor_offsets[0]]).astype(jnp.int32)
    attended = attend_all(ids, queries, near, far, heads, head_dim)
    arrived = lax.all_to_all(attended, "frame", 0, 0).reshape(count * heads * head_dim, rows)
    arrived_far = swapped(arrived, "head")

    columns = w_out.shape[1] // 2
    w_part = lax.dynamic_slice_in_dim(w_out.T, group * columns, columns, 0)
    w_part = after(w_part, near[-1])
    w_part = lax.all_to_all(jnp.broadcast_to(w_part[None], (count, *w_part.shape)), "frame", 0, 0)
    w_other = swapped(w_part, "groups")
    near_sum = add_part(where, w_part, w_other, arrived, frame_part, gate_part, jnp.float32)
    w_far = [swapped(w, "head") for w in (w_part, w_other)]
    updated = add_part(where, *w_far, arrived_far, near_sum, gate_part, jnp.bfloat16)
    return updated.T[None]


def on_device(frames, modulation, w_qkv, w_out, anchor_offsets):
    count = lax.axis_size("frame")
    fits = (
        frames.shape[0] == 1
        and anchor_offsets.shape[0] == 1
        and count == 4
        and lax.axis_size("groups") == 2
        and lax.axis_size("head") == 2
        and lax.axis_size("tok") == 2
        and w_qkv.shape[1] == 2 * count
        and w_qkv.shape[3] % 8 == 0
        and frames.shape[1] % 256 == 0
        and frames.shape[2] % 32 == 0
    )
    step = by_heads if fits else by_frames
    return step(frames, modulation, w_qkv, w_out, anchor_offsets)


def solution(mesh):
    placed = (
        P(("groups", "frame"), "tok", None),
        P(),
        P("frame", "head", None, None),
        P("head", "frame"),
        P("groups"),
    )
    return jax.shard_map(
        on_device,
        mesh=mesh,
        in_specs=placed,
        out_specs=P(("groups", "frame"), "tok", "head"),
        check_vma=False,
    )
```

```python
import functools
import math

import jax
import jax.numpy as jnp
from jax import lax
from jax.experimental import pallas as pl
from jax.experimental.pallas import tpu as pltpu
from jax.sharding import PartitionSpec as P

MIB = 2**20


def dot_nn(a, b):
    return lax.dot_general(a, b, (((1,), (0,)), ((), ())), preferred_element_type=jnp.float32)


def dot_nt(a, b):
    return lax.dot_general(a, b, (((1,), (1,)), ((), ())), preferred_element_type=jnp.float32)


def call(kernel, out_shape, operands, scratch=(), flops=0, moved=0, left=(), grant=8):
    smem = pl.BlockSpec(memory_space=pltpu.SMEM)
    vmem = pl.BlockSpec(memory_space=pltpu.VMEM)
    where = pl.BlockSpec(memory_space=pl.ANY)
    many = isinstance(out_shape, (list, tuple))
    return pl.pallas_call(
        kernel,
        out_shape=out_shape,
        in_specs=[where if i in left else smem if x.dtype == jnp.int32 else vmem for i, x in enumerate(operands)],
        out_specs=[vmem] * len(out_shape) if many else vmem,
        scratch_shapes=list(scratch),
        compiler_params=pltpu.CompilerParams(vmem_limit_bytes=grant * MIB),
        cost_estimate=pl.CostEstimate(flops=flops, bytes_accessed=moved, transcendentals=0),
    )(*operands)


def norm_kernel(place_ref, frame_ref, mod_ref, out_ref, rows, arrived):
    half = out_ref.shape[0]
    start = pl.multiple_of(place_ref[0] * half, half)
    copy = pltpu.make_async_copy(frame_ref.at[pl.ds(start, half), :], rows, arrived)
    copy.start()
    copy.wait()
    values = rows[...].astype(jnp.float32)
    row_mean = jnp.mean(values, axis=-1, keepdims=True)
    centred = values - row_mean
    row_var = jnp.mean(centred * centred, axis=-1, keepdims=True)
    normed = centred * lax.rsqrt(row_var + 1e-06)
    out_ref[...] = (normed * (1.0 + mod_ref[1:2, :]) + mod_ref[0:1, :]).astype(jnp.bfloat16)


def norm_half(place, frame, modulation):
    half, width = frame.shape[0] // 2, frame.shape[1]
    return call(
        norm_kernel,
        jax.ShapeDtypeStruct((half, width), jnp.bfloat16),
        (place, frame, modulation),
        [pltpu.VMEM((half, width), jnp.bfloat16), pltpu.SemaphoreType.DMA],
        flops=20 * half * width,
        moved=4 * half * width,
        left=(1,),
    )


def weight_kernel(heads, head_dim, parts_ref, out_ref):
    _, count, share, part_rows = parts_ref.shape
    head_rows = 3 * head_dim
    per_head = []
    for head in range(heads):
        low, high = [
            jnp.concatenate([parts_ref[head * 2 + i, source] for source in range(count)], 0).astype(jnp.float32).T
            for i in range(2)
        ]
        per_head.append(jnp.concatenate([low, high[2 * part_rows - head_rows :]], 0))
    rows = [w[kind * head_dim : (kind + 1) * head_dim] for kind in (1, 2, 0) for w in per_head]
    out_ref[...] = jnp.concatenate(rows, 0).astype(jnp.bfloat16)


def join_weight(parts, heads, head_dim):
    _, count, share, _ = parts.shape
    return call(
        functools.partial(weight_kernel, heads, head_dim),
        jax.ShapeDtypeStruct((heads * 3 * head_dim, count * share), jnp.bfloat16),
        (parts,),
        grant=16,
    )


def project_kernel(kv_width, place_ref, weight_ref, mine_ref, other_ref, kv_ref, *q_refs):
    half = mine_ref.shape[0]
    for part, ref in ((place_ref[0], mine_ref), (1 - place_ref[0], other_ref)):
        span = pl.ds(pl.multiple_of(part * half, half), half)
        mixed = dot_nt(weight_ref[...] if q_refs else weight_ref[:kv_width], ref[...]).astype(jnp.bfloat16)
        kv_ref[:, span] = mixed[:kv_width]
        for q_ref in q_refs:
            q_ref[:, span] = mixed[kv_width:]


def project(place, weight, mine, other, kv_width, with_queries=True):
    half, width = mine.shape
    rows = 2 * half
    out_width = weight.shape[0]
    return call(
        functools.partial(project_kernel, kv_width),
        (
            jax.ShapeDtypeStruct((kv_width, rows), jnp.bfloat16),
            jax.ShapeDtypeStruct((out_width - kv_width, rows), jnp.bfloat16),
        )[: 2 if with_queries else 1],
        (place, weight, mine, other),
        flops=2 * rows * width * out_width,
        moved=2 * (rows * width + width * out_width + rows * out_width),
    )


def unpack_queries(ref, frame, heads, head_dim, q_all):
    queries = ref[...].astype(jnp.float32)
    for head in range(heads):
        q_all[frame * heads + head] = queries[head * head_dim : (head + 1) * head_dim].astype(jnp.bfloat16)


def unpack_keyvals(ref, base, side, heads, head_dim, k_all, v_all):
    rows = ref.shape[1]
    ones = jnp.ones((v_all.shape[1] - head_dim, rows), jnp.float32)
    keyvals = ref[...].astype(jnp.float32)
    span = pl.ds(side * rows, rows)
    for head in range(heads):
        keys = keyvals[head * head_dim : (head + 1) * head_dim]
        k_all[base + head, span, :] = keys.T.astype(jnp.bfloat16)
        first = (heads + head) * head_dim
        values = jnp.concatenate([keyvals[first : first + head_dim], ones], 0)
        v_all[base + head, :, span] = values.astype(jnp.bfloat16)


def run_items(items, q_list, k_list, key_rows, heads, head_dim, q_all, k_all, v_all, scores_of, block_high, scale_old, high, total):
    factor = math.log2(math.e) / math.sqrt(head_dim)
    step = math.gcd(key_rows, 256)

    def stage(now, before):
        if now is not None:
            head_a, item_a = now
            state_a = q_list[item_a] * heads + head_a
            key_a = k_list[item_a] * heads + head_a
            queries = q_all[state_a]
            old = high[state_a]
            top = old
        if before is not None:
            head_b, item_b = before
            state_b = q_list[item_b] * heads + head_b
            key_b = k_list[item_b] * heads + head_b
            top_b = block_high[head_b]
            running = total[state_b] * scale_old[head_b]
        for start in range(0, key_rows, step):
            part = pl.ds(start, step)
            if now is not None:
                scores = dot_nn(k_all[key_a, part, :], queries)
                scores_of[head_a][part, :] = scores
                top = jnp.maximum(top, jnp.max(scores, axis=0, keepdims=True))
            if before is not None:
                probs = jnp.exp2((scores_of[head_b][part, :] - top_b) * factor).astype(jnp.bfloat16)
                running = running + dot_nn(v_all[key_b, :, part], probs)
        if before is not None:
            total[state_b] = running
        if now is not None:
            scale_old[head_a] = jnp.exp2((old - top) * factor)
            block_high[head_a] = top
            high[state_a] = top

    def body(index, carry):
        stage((1, index), (0, index))
        stage((0, index + 1), (1, index))
        return carry

    stage((0, 0), None)
    lax.fori_loop(0, items - 1, body, 0)
    stage((1, items - 1), (0, items - 1))
    stage(None, (1, items - 1))


def list_items(count, anchor, keep, q_list, k_list):
    items = jnp.int32(0)
    for frame in range(count):
        pairs = [(jnp.int32(frame), None)]
        if frame > 0:
            pairs.append((jnp.int32(frame - 1), None))
        pairs.append((anchor, (anchor != frame) & (anchor != frame - 1)))
        for key, valid in pairs:
            q_list[items] = frame
            k_list[items] = key
            kept = keep(frame, key)
            items += jnp.where(kept if valid is None else kept & valid, 1, 0)
    return items


def first_kernel(count, heads, head_dim, *refs):
    ids_ref = refs[0]
    q_refs = refs[1 : 1 + count]
    near_refs = refs[1 + count : 1 + 2 * count]
    far_refs = refs[1 + 2 * count : 3 * count]
    high, total = refs[3 * count : 3 * count + 2]
    q_all, k_all, v_all, even, odd, block_high, scale_old, q_list, k_list = refs[3 * count + 2 :]
    rows = q_refs[0].shape[1]
    for slot in range(count):
        frame = ids_ref[slot]
        unpack_queries(q_refs[slot], frame, heads, head_dim, q_all)
        unpack_keyvals(near_refs[slot], frame * heads, 0, heads, head_dim, k_all, v_all)
        if slot < count - 1:
            unpack_keyvals(far_refs[slot], frame * heads, 1, heads, head_dim, k_all, v_all)
    anchor = ids_ref[count]
    late = ids_ref[count - 1]
    high[...] = jnp.full_like(high, -1e30)
    total[...] = jnp.zeros_like(total)
    rest = (heads, head_dim, q_all, k_all, v_all, (even, odd), block_high, scale_old, high, total)
    items = list_items(count, anchor, lambda q, k: k != late, q_list, k_list)
    run_items(items, q_list, k_list, 2 * rows, *rest)
    items = list_items(count, anchor, lambda q, k: k == late, q_list, k_list)
    run_items(items, q_list, k_list, rows, *rest)


def second_kernel(count, heads, head_dim, *refs):
    ids_ref = refs[0]
    q_refs = refs[1 : 1 + count]
    far_ref, high_in, total_in, out_ref = refs[1 + count : 5 + count]
    high, total, q_all, k_late, v_late, even, odd, block_high, scale_old, q_list, k_list = refs[5 + count :]
    rows = q_refs[0].shape[1]
    for slot in range(count):
        unpack_queries(q_refs[slot], ids_ref[slot], heads, head_dim, q_all)
    unpack_keyvals(far_ref, 0, 0, heads, head_dim, k_late, v_late)
    high[...] = high_in[...]
    total[...] = total_in[...]
    late = ids_ref[count - 1]
    items = list_items(count, ids_ref[count], lambda q, k: k == late, q_list, k_list)
    for item in range(count):
        k_list[item] = 0
    run_items(
        items, q_list, k_list, rows, heads, head_dim, q_all, k_late, v_late, (even, odd), block_high, scale_old, high, total
    )
    for frame in range(count):
        parts = []
        for head in range(heads):
            sums = total[frame * heads + head]
            parts.append(sums[:head_dim] / sums[head_dim : head_dim + 1])
        out_ref[frame] = jnp.concatenate(parts, 0).astype(jnp.bfloat16)


def attend_all(ids, queries, near, far, heads, head_dim):
    count = len(queries)
    rows = queries[0].shape[1]
    value_rows = head_dim + 8
    states = count * heads
    f32 = jnp.float32
    lists = [pltpu.SMEM((3 * count + 1,), jnp.int32)] * 2
    tops = [pltpu.VMEM((heads, 1, rows), f32)] * 2
    state = (
        jax.ShapeDtypeStruct((states, 1, rows), f32),
        jax.ShapeDtypeStruct((states, value_rows, rows), f32),
    )
    high, total = call(
        functools.partial(first_kernel, count, heads, head_dim),
        state,
        (ids, *queries, *near, *far[:-1]),
        [
            pltpu.VMEM((states, head_dim, rows), jnp.bfloat16),
            pltpu.VMEM((states, 2 * rows, head_dim), jnp.bfloat16),
            pltpu.VMEM((states, value_rows, 2 * rows), jnp.bfloat16),
            pltpu.VMEM((2 * rows, rows), f32),
            pltpu.VMEM((2 * rows, rows), f32),
            *tops,
            *lists,
        ],
        flops=3 * count * heads * rows * 2 * rows * head_dim * 16,
        moved=2 * count * heads * head_dim * rows * 6,
        grant=24,
    )
    return call(
        functools.partial(second_kernel, count, heads, head_dim),
        jax.ShapeDtypeStruct((count, heads * head_dim, rows), jnp.bfloat16),
        (ids, *queries, far[-1], high, total),
        [
            pltpu.VMEM(state[0].shape, f32),
            pltpu.VMEM(state[1].shape, f32),
            pltpu.VMEM((states, head_dim, rows), jnp.bfloat16),
            pltpu.VMEM((heads, rows, head_dim), jnp.bfloat16),
            pltpu.VMEM((heads, value_rows, rows), jnp.bfloat16),
            pltpu.VMEM((rows, rows), f32),
            pltpu.VMEM((rows, rows), f32),
            *tops,
            *lists,
        ],
        flops=heads * rows * rows * head_dim * 16,
        moved=2 * count * heads * head_dim * rows * 6,
        grant=16,
    )


def residual_kernel(core_ref, frame_ref, mod_ref, out_ref, gate_ref):
    width = out_ref.shape[0]
    frame = frame_ref[...].astype(jnp.float32)
    mine = jnp.where(core_ref[0] == 0, frame[:, :width], frame[:, width:])
    out_ref[...] = mine.T.astype(jnp.bfloat16)
    gate = jnp.broadcast_to(mod_ref[2:3, :], (8, 2 * width))
    gate = jnp.where(core_ref[0] == 0, gate[:, :width], gate[:, width:])
    gate_ref[...] = gate.T


def residual(core, frame, modulation):
    rows, width = frame.shape
    return call(
        residual_kernel,
        (jax.ShapeDtypeStruct((width // 2, rows), jnp.bfloat16), jax.ShapeDtypeStruct((width // 2, 8), jnp.float32)),
        (core, frame, modulation),
        flops=4 * rows * width,
        moved=3 * rows * width,
        grant=16,
    )


def part_kernel(where_ref, mine_ref, other_ref, heads_ref, start_ref, gate_ref, out_ref):
    group, core = where_ref[1], where_ref[3]
    block = mine_ref.shape[1]
    per_core = mine_ref.shape[0] // 2
    for same, ref in ((True, mine_ref), (False, other_ref)):
        half = group if same else 1 - group
        for index in range(per_core):
            rows = pl.ds(pl.multiple_of((index * 2 + half) * block, block), block)
            projected = dot_nn(ref[core * per_core + index], heads_ref[...])
            updated = start_ref[rows, :].astype(jnp.float32) + gate_ref[rows, 0:1] * projected
            out_ref[rows, :] = updated.astype(out_ref.dtype)


def add_part(where, mine, other, heads, start, gate, dtype):
    return call(
        part_kernel,
        jax.ShapeDtypeStruct(start.shape, dtype),
        (where, mine, other, heads, start, gate),
        grant=16,
    )


def swapped(block, axis):
    return lax.ppermute(block, axis, [(0, 1), (1, 0)])


def shifted(block, axis, distance):
    devices = range(lax.axis_size(axis))
    route = [(i - distance, i) for i in devices if i - distance in devices]
    return lax.ppermute(block, axis, route)


def from_partner(block, axis, stride):
    count = lax.axis_size(axis)
    route = []
    for low in range(count):
        high = low | 1 << stride
        if high != low and high < count:
            route += [(low, high), (high, low)]
    return lax.ppermute(block, axis, route)


def attend(queries, kv_all, first_frame, anchor, head_dim):
    frame_count, query_rows, query_width = queries.shape
    key_count = kv_all.shape[1]
    head_count = query_width // head_dim
    block_rows = math.gcd(512, query_rows)
    kv_heads = kv_all.reshape(frame_count + 2, key_count, head_count, 2, head_dim)
    global_idx = first_frame + 0
    use_prev = global_idx > 0
    use_anchor = (anchor != global_idx) & (anchor != global_idx - 1)
    valid_keys = jnp.concatenate(
        [
            jnp.broadcast_to(use_anchor, (key_count,)),
            jnp.broadcast_to(use_prev, (key_count,)),
            jnp.ones((key_count,), bool),
        ]
    )
    frame_queries = queries[0]

    def one_head(head_idx):
        picked = lax.dynamic_index_in_dim(kv_heads, head_idx, 2, keepdims=False)
        key_rows = jnp.concatenate(
            [picked[frame_count + 1, :, 0], picked[frame_count, :, 0], picked[0, :, 0]], 0
        )
        val_rows = jnp.concatenate(
            [picked[frame_count + 1, :, 1], picked[frame_count, :, 1], picked[0, :, 1]], 0
        )
        query_head = lax.dynamic_slice_in_dim(frame_queries, head_idx * head_dim, head_dim, 1)
        query_blocks = query_head.reshape(query_rows // block_rows, block_rows, head_dim)

        def one_block(query_block):
            scores = lax.dot_general(
                query_block, key_rows, (((1,), (1,)), ((), ())), preferred_element_type=jnp.float32
            ) * head_dim ** (-0.5)
            scores = jnp.where(valid_keys[None, :], scores, -1e30)
            row_max = jnp.max(scores, axis=-1, keepdims=True)
            probs = jnp.exp(scores - row_max)
            denominator = jnp.sum(probs, axis=-1, keepdims=True)
            numerator = jnp.dot(
                probs.astype(jnp.bfloat16), val_rows, preferred_element_type=jnp.float32
            )
            return (numerator / denominator).astype(jnp.bfloat16)

        return lax.map(one_block, query_blocks).reshape(query_rows, head_dim)

    per_head = lax.map(one_head, jnp.arange(head_count, dtype=jnp.int32))
    frame_outputs = [jnp.transpose(per_head, (1, 0, 2)).reshape(query_rows, head_count * head_dim)]
    return jnp.stack(frame_outputs)


def by_frames(frames, modulation, w_qkv, w_out, anchor_offsets):
    frame_count, row_count, model_width = frames.shape
    head_local = w_qkv.shape[1]
    head_dim = w_qkv.shape[3]
    my_index = lax.axis_index("frame")
    flat_rows = frames.reshape(frame_count * row_count, model_width).astype(jnp.float32)
    row_mean = jnp.mean(flat_rows, axis=-1, keepdims=True)
    centred = flat_rows - row_mean
    row_var = jnp.mean(centred * centred, axis=-1, keepdims=True)
    normed = centred * lax.rsqrt(row_var + 1e-06)
    hidden = (normed * (1.0 + modulation[1]) + modulation[0]).astype(jnp.bfloat16)
    full_weight = lax.all_gather(w_qkv, "frame", axis=0, tiled=True)
    mixed = jnp.dot(
        hidden,
        full_weight.reshape(model_width, head_local * 3 * head_dim),
        preferred_element_type=jnp.float32,
    )
    mixed = mixed.astype(jnp.bfloat16).reshape(frame_count, row_count, head_local, 3, head_dim)
    queries = mixed[:, :, :, 0, :].reshape(frame_count, row_count, head_local * head_dim)
    keyvals = mixed[:, :, :, 1:, :].reshape(frame_count, row_count, head_local * 2 * head_dim)
    span_count = anchor_offsets.shape[0]
    total_frames = frame_count * lax.axis_size("frame")
    span_len = total_frames // span_count
    first_frame = my_index * frame_count
    mine_span = first_frame // span_len
    anchor = mine_span * span_len + anchor_offsets[mine_span]
    prev_kv = shifted(keyvals[frame_count - 1], "frame", 1)
    holder = anchor // frame_count
    anchor_kv = lax.dynamic_index_in_dim(keyvals, anchor % frame_count, 0, keepdims=False)
    levels = (span_len // frame_count).bit_length() - 1
    for bit_index in range(levels):
        partner = from_partner(anchor_kv, "frame", bit_index)
        take_partner = my_index >> bit_index & 1 != holder >> bit_index & 1
        anchor_kv = jnp.where(take_partner, partner, anchor_kv)
    kv_all = jnp.concatenate([keyvals, prev_kv[None], anchor_kv[None]], 0)
    kv_whole = lax.all_gather(kv_all, "tok", axis=1, tiled=True)
    attended = attend(queries, kv_whole, first_frame, anchor, head_dim)
    flat_attended = attended.reshape(frame_count * row_count, head_local * head_dim)
    term_cols = jnp.dot(
        flat_attended,
        lax.all_gather(w_out, "frame", axis=1, tiled=True),
        preferred_element_type=jnp.float32,
    )
    summed = lax.psum_scatter(term_cols, "head", scatter_dimension=1, tiled=True)
    half_width = summed.shape[1]
    col_start = lax.axis_index("head") * half_width
    residual_in = lax.dynamic_slice_in_dim(flat_rows, col_start, half_width, 1)
    gate_part = lax.dynamic_slice_in_dim(modulation[2], col_start, half_width, 0)
    result = (residual_in + gate_part * summed).astype(jnp.bfloat16)
    return result.reshape(frame_count, row_count, half_width)


def flipped(block, axis, distance):
    return lax.ppermute(block, axis, [(i, i ^ distance) for i in range(lax.axis_size(axis))])


def after(block, other):
    return lax.optimization_barrier((block, other))[0]


def by_heads(frames, modulation, w_qkv, w_out, anchor_offsets):
    _, rows, width = frames.shape
    share, head_local, _, head_dim = w_qkv.shape
    count = lax.axis_size("frame")
    heads = head_local // count
    core = lax.axis_index("head")
    me = lax.axis_index("frame")
    group = lax.axis_index("groups")
    frame = frames[0]
    place = core.reshape(1).astype(jnp.int32)

    tok = lax.axis_index("tok")
    where = jnp.stack([me, group, tok, core]).astype(jnp.int32)

    blocks = jnp.transpose(w_qkv, (1, 2, 3, 0)).reshape(count, heads, 3 * head_dim, share)
    part_rows = -(-3 * head_dim // 32) * 16
    start = tok * (3 * head_dim - part_rows)
    part = lax.dynamic_slice(blocks, (0, group, start, 0), (count, 1, part_rows, share))[:, 0]
    part = jnp.transpose(part, (0, 2, 1))
    part = lax.all_to_all(part, "frame", 0, 0)
    plane = lax.all_to_all(jnp.broadcast_to(part[None], (4, *part.shape)), ("groups", "tok"), 0, 0)
    weight = join_weight(plane, heads, head_dim)
    kv_width = 2 * heads * head_dim

    mine = norm_half(place, frame, modulation)
    arrivals = [mine, flipped(mine, "frame", 1), flipped(mine, "frame", 2)]
    arrivals.append(flipped(arrivals[2], "frame", 1))
    frame_part, gate_part = residual(place, after(frame, arrivals[1]), modulation)

    queries, near, far = [], [], []
    for distance, block in enumerate(arrivals):
        if distance == 3:
            block = after(block, (frame_part, near[0], near[1], near[2]))
        kv, q = project(place, weight, block, swapped(block, "head"), kv_width)
        queries.append(q)
        near.append(kv)
        if distance == 0:
            across = after(swapped(block, "tok"), kv)
            far += project(place, weight, across, swapped(across, "head"), kv_width, False)
        else:
            far.append(swapped(kv, "tok"))
    ids = jnp.stack([me ^ distance for distance in range(count)] + [anchor_offsets[0]]).astype(jnp.int32)
    attended = attend_all(ids, queries, near, far, heads, head_dim)
    arrived = lax.all_to_all(attended, "frame", 0, 0).reshape(count * heads * head_dim, rows)
    arrived_far = swapped(arrived, "head")

    columns = w_out.shape[1] // 2
    w_part = lax.dynamic_slice_in_dim(w_out.T, group * columns, columns, 0)
    w_part = after(w_part, near[-1])
    w_part = lax.all_to_all(jnp.broadcast_to(w_part[None], (count, *w_part.shape)), "frame", 0, 0)
    w_other = swapped(w_part, "groups")
    near_sum = add_part(where, w_part, w_other, arrived, frame_part, gate_part, jnp.float32)
    w_far = [swapped(w, "head") for w in (w_part, w_other)]
    updated = add_part(where, *w_far, arrived_far, near_sum, gate_part, jnp.bfloat16)
    return updated.T[None]


def on_device(frames, modulation, w_qkv, w_out, anchor_offsets):
    count = lax.axis_size("frame")
    fits = (
        frames.shape[0] == 1
        and anchor_offsets.shape[0] == 1
        and count == 4
        and lax.axis_size("groups") == 2
        and lax.axis_size("head") == 2
        and lax.axis_size("tok") == 2
        and w_qkv.shape[1] == 2 * count
        and w_qkv.shape[3] % 8 == 0
        and frames.shape[1] % 256 == 0
        and frames.shape[2] % 32 == 0
    )
    step = by_heads if fits else by_frames
    return step(frames, modulation, w_qkv, w_out, anchor_offsets)


def solution(mesh):
    placed = (
        P(("groups", "frame"), "tok", None),
        P(),
        P("frame", "head", None, None),
        P("head", "frame"),
        P("groups"),
    )
    return jax.shard_map(
        on_device,
        mesh=mesh,
        in_specs=placed,
        out_specs=P(("groups", "frame"), "tok", "head"),
        check_vma=False,
    )
```

```python
import functools
import math

import jax
import jax.numpy as jnp
from jax import lax
from jax.experimental import pallas as pl
from jax.experimental.pallas import tpu as pltpu
from jax.sharding import PartitionSpec as P

MIB = 2**20


def dot_nn(a, b):
    return lax.dot_general(a, b, (((1,), (0,)), ((), ())), preferred_element_type=jnp.float32)


def dot_nt(a, b):
    return lax.dot_general(a, b, (((1,), (1,)), ((), ())), preferred_element_type=jnp.float32)


def call(kernel, out_shape, operands, scratch=(), flops=0, moved=0, left=(), grant=8):
    smem = pl.BlockSpec(memory_space=pltpu.SMEM)
    vmem = pl.BlockSpec(memory_space=pltpu.VMEM)
    where = pl.BlockSpec(memory_space=pl.ANY)
    many = isinstance(out_shape, (list, tuple))
    return pl.pallas_call(
        kernel,
        out_shape=out_shape,
        in_specs=[where if i in left else smem if x.dtype == jnp.int32 else vmem for i, x in enumerate(operands)],
        out_specs=[vmem] * len(out_shape) if many else vmem,
        scratch_shapes=list(scratch),
        compiler_params=pltpu.CompilerParams(vmem_limit_bytes=grant * MIB),
        cost_estimate=pl.CostEstimate(flops=flops, bytes_accessed=moved, transcendentals=0),
    )(*operands)


def norm_kernel(place_ref, frame_ref, mod_ref, out_ref, rows, arrived):
    half = out_ref.shape[0]
    start = pl.multiple_of(place_ref[0] * half, half)
    copy = pltpu.make_async_copy(frame_ref.at[pl.ds(start, half), :], rows, arrived)
    copy.start()
    copy.wait()
    values = rows[...].astype(jnp.float32)
    row_mean = jnp.mean(values, axis=-1, keepdims=True)
    centred = values - row_mean
    row_var = jnp.mean(centred * centred, axis=-1, keepdims=True)
    normed = centred * lax.rsqrt(row_var + 1e-06)
    out_ref[...] = (normed * (1.0 + mod_ref[1:2, :]) + mod_ref[0:1, :]).astype(jnp.bfloat16)


def norm_half(place, frame, modulation):
    half, width = frame.shape[0] // 2, frame.shape[1]
    return call(
        norm_kernel,
        jax.ShapeDtypeStruct((half, width), jnp.bfloat16),
        (place, frame, modulation),
        [pltpu.VMEM((half, width), jnp.bfloat16), pltpu.SemaphoreType.DMA],
        flops=20 * half * width,
        moved=4 * half * width,
        left=(1,),
    )


def weight_kernel(heads, head_dim, parts_ref, out_ref):
    _, count, share, part_rows = parts_ref.shape
    head_rows = 3 * head_dim
    per_head = []
    for head in range(heads):
        low, high = [
            jnp.concatenate([parts_ref[head * 2 + i, source] for source in range(count)], 0).astype(jnp.float32).T
            for i in range(2)
        ]
        per_head.append(jnp.concatenate([low, high[2 * part_rows - head_rows :]], 0))
    rows = [w[kind * head_dim : (kind + 1) * head_dim] for kind in (1, 2, 0) for w in per_head]
    out_ref[...] = jnp.concatenate(rows, 0).astype(jnp.bfloat16)


def join_weight(parts, heads, head_dim):
    _, count, share, _ = parts.shape
    return call(
        functools.partial(weight_kernel, heads, head_dim),
        jax.ShapeDtypeStruct((heads * 3 * head_dim, count * share), jnp.bfloat16),
        (parts,),
        grant=16,
    )


def project_kernel(kv_width, place_ref, weight_ref, mine_ref, other_ref, kv_ref, *q_refs):
    half = mine_ref.shape[0]
    for part, ref in ((place_ref[0], mine_ref), (1 - place_ref[0], other_ref)):
        span = pl.ds(pl.multiple_of(part * half, half), half)
        mixed = dot_nt(weight_ref[...] if q_refs else weight_ref[:kv_width], ref[...]).astype(jnp.bfloat16)
        kv_ref[:, span] = mixed[:kv_width]
        for q_ref in q_refs:
            q_ref[:, span] = mixed[kv_width:]


def project(place, weight, mine, other, kv_width, with_queries=True):
    half, width = mine.shape
    rows = 2 * half
    out_width = weight.shape[0]
    return call(
        functools.partial(project_kernel, kv_width),
        (
            jax.ShapeDtypeStruct((kv_width, rows), jnp.bfloat16),
            jax.ShapeDtypeStruct((out_width - kv_width, rows), jnp.bfloat16),
        )[: 2 if with_queries else 1],
        (place, weight, mine, other),
        flops=2 * rows * width * out_width,
        moved=2 * (rows * width + width * out_width + rows * out_width),
    )


def unpack_queries(ref, frame, heads, head_dim, q_all):
    queries = ref[...].astype(jnp.float32)
    for head in range(heads):
        q_all[frame * heads + head] = queries[head * head_dim : (head + 1) * head_dim].astype(jnp.bfloat16)


def unpack_keyvals(ref, base, side, heads, head_dim, k_all, v_all):
    rows = ref.shape[1]
    ones = jnp.ones((v_all.shape[1] - head_dim, rows), jnp.float32)
    keyvals = ref[...].astype(jnp.float32)
    span = pl.ds(side * rows, rows)
    for head in range(heads):
        keys = keyvals[head * head_dim : (head + 1) * head_dim]
        k_all[base + head, span, :] = keys.T.astype(jnp.bfloat16)
        first = (heads + head) * head_dim
        values = jnp.concatenate([keyvals[first : first + head_dim], ones], 0)
        v_all[base + head, :, span] = values.astype(jnp.bfloat16)


def run_items(items, q_list, k_list, key_rows, heads, head_dim, q_all, k_all, v_all, scores_of, block_high, scale_old, high, total):
    factor = math.log2(math.e) / math.sqrt(head_dim)
    step = math.gcd(key_rows, 512)

    def stage(now, before):
        if now is not None:
            head_a, item_a = now
            state_a = q_list[item_a] * heads + head_a
            key_a = k_list[item_a] * heads + head_a
            queries = q_all[state_a]
            old = high[state_a]
            top = old
        if before is not None:
            head_b, item_b = before
            state_b = q_list[item_b] * heads + head_b
            key_b = k_list[item_b] * heads + head_b
            top_b = block_high[head_b]
            running = total[state_b] * scale_old[head_b]
        for start in range(0, key_rows, step):
            part = pl.ds(start, step)
            if now is not None:
                scores = dot_nn(k_all[key_a, part, :], queries)
                scores_of[head_a][part, :] = scores
                top = jnp.maximum(top, jnp.max(scores, axis=0, keepdims=True))
            if before is not None:
                probs = jnp.exp2((scores_of[head_b][part, :] - top_b) * factor).astype(jnp.bfloat16)
                running = running + dot_nn(v_all[key_b, :, part], probs)
        if before is not None:
            total[state_b] = running
        if now is not None:
            scale_old[head_a] = jnp.exp2((old - top) * factor)
            block_high[head_a] = top
            high[state_a] = top

    def body(index, carry):
        stage((1, index), (0, index))
        stage((0, index + 1), (1, index))
        return carry

    stage((0, 0), None)
    lax.fori_loop(0, items - 1, body, 0)
    stage((1, items - 1), (0, items - 1))
    stage(None, (1, items - 1))


def list_items(count, anchor, keep, q_list, k_list):
    items = jnp.int32(0)
    for frame in range(count):
        pairs = [(jnp.int32(frame), None)]
        if frame > 0:
            pairs.append((jnp.int32(frame - 1), None))
        pairs.append((anchor, (anchor != frame) & (anchor != frame - 1)))
        for key, valid in pairs:
            q_list[items] = frame
            k_list[items] = key
            kept = keep(frame, key)
            items += jnp.where(kept if valid is None else kept & valid, 1, 0)
    return items


def first_kernel(count, heads, head_dim, *refs):
    ids_ref = refs[0]
    q_refs = refs[1 : 1 + count]
    near_refs = refs[1 + count : 1 + 2 * count]
    far_refs = refs[1 + 2 * count : 3 * count]
    high, total = refs[3 * count : 3 * count + 2]
    q_all, k_all, v_all, even, odd, block_high, scale_old, q_list, k_list = refs[3 * count + 2 :]
    rows = q_refs[0].shape[1]
    for slot in range(count):
        frame = ids_ref[slot]
        unpack_queries(q_refs[slot], frame, heads, head_dim, q_all)
        unpack_keyvals(near_refs[slot], frame * heads, 0, heads, head_dim, k_all, v_all)
        if slot < count - 1:
            unpack_keyvals(far_refs[slot], frame * heads, 1, heads, head_dim, k_all, v_all)
    anchor = ids_ref[count]
    late = ids_ref[count - 1]
    high[...] = jnp.full_like(high, -1e30)
    total[...] = jnp.zeros_like(total)
    rest = (heads, head_dim, q_all, k_all, v_all, (even, odd), block_high, scale_old, high, total)
    items = list_items(count, anchor, lambda q, k: k != late, q_list, k_list)
    run_items(items, q_list, k_list, 2 * rows, *rest)
    items = list_items(count, anchor, lambda q, k: k == late, q_list, k_list)
    run_items(items, q_list, k_list, rows, *rest)


def second_kernel(count, heads, head_dim, *refs):
    ids_ref = refs[0]
    q_refs = refs[1 : 1 + count]
    far_ref, high_in, total_in, out_ref = refs[1 + count : 5 + count]
    high, total, q_all, k_late, v_late, even, odd, block_high, scale_old, q_list, k_list = refs[5 + count :]
    rows = q_refs[0].shape[1]
    for slot in range(count):
        unpack_queries(q_refs[slot], ids_ref[slot], heads, head_dim, q_all)
    unpack_keyvals(far_ref, 0, 0, heads, head_dim, k_late, v_late)
    high[...] = high_in[...]
    total[...] = total_in[...]
    late = ids_ref[count - 1]
    items = list_items(count, ids_ref[count], lambda q, k: k == late, q_list, k_list)
    for item in range(count):
        k_list[item] = 0
    run_items(
        items, q_list, k_list, rows, heads, head_dim, q_all, k_late, v_late, (even, odd), block_high, scale_old, high, total
    )
    for frame in range(count):
        parts = []
        for head in range(heads):
            sums = total[frame * heads + head]
            parts.append(sums[:head_dim] / sums[head_dim : head_dim + 1])
        out_ref[frame] = jnp.concatenate(parts, 0).astype(jnp.bfloat16)


def attend_all(ids, queries, near, far, heads, head_dim):
    count = len(queries)
    rows = queries[0].shape[1]
    value_rows = head_dim + 8
    states = count * heads
    f32 = jnp.float32
    lists = [pltpu.SMEM((3 * count + 1,), jnp.int32)] * 2
    tops = [pltpu.VMEM((heads, 1, rows), f32)] * 2
    state = (
        jax.ShapeDtypeStruct((states, 1, rows), f32),
        jax.ShapeDtypeStruct((states, value_rows, rows), f32),
    )
    high, total = call(
        functools.partial(first_kernel, count, heads, head_dim),
        state,
        (ids, *queries, *near, *far[:-1]),
        [
            pltpu.VMEM((states, head_dim, rows), jnp.bfloat16),
            pltpu.VMEM((states, 2 * rows, head_dim), jnp.bfloat16),
            pltpu.VMEM((states, value_rows, 2 * rows), jnp.bfloat16),
            pltpu.VMEM((2 * rows, rows), f32),
            pltpu.VMEM((2 * rows, rows), f32),
            *tops,
            *lists,
        ],
        flops=3 * count * heads * rows * 2 * rows * head_dim * 16,
        moved=2 * count * heads * head_dim * rows * 6,
        grant=24,
    )
    return call(
        functools.partial(second_kernel, count, heads, head_dim),
        jax.ShapeDtypeStruct((count, heads * head_dim, rows), jnp.bfloat16),
        (ids, *queries, far[-1], high, total),
        [
            pltpu.VMEM(state[0].shape, f32),
            pltpu.VMEM(state[1].shape, f32),
            pltpu.VMEM((states, head_dim, rows), jnp.bfloat16),
            pltpu.VMEM((heads, rows, head_dim), jnp.bfloat16),
            pltpu.VMEM((heads, value_rows, rows), jnp.bfloat16),
            pltpu.VMEM((rows, rows), f32),
            pltpu.VMEM((rows, rows), f32),
            *tops,
            *lists,
        ],
        flops=heads * rows * rows * head_dim * 16,
        moved=2 * count * heads * head_dim * rows * 6,
        grant=16,
    )


def residual_kernel(core_ref, frame_ref, mod_ref, out_ref, gate_ref):
    width = out_ref.shape[0]
    frame = frame_ref[...].astype(jnp.float32)
    mine = jnp.where(core_ref[0] == 0, frame[:, :width], frame[:, width:])
    out_ref[...] = mine.T.astype(jnp.bfloat16)
    gate = jnp.broadcast_to(mod_ref[2:3, :], (8, 2 * width))
    gate = jnp.where(core_ref[0] == 0, gate[:, :width], gate[:, width:])
    gate_ref[...] = gate.T


def residual(core, frame, modulation):
    rows, width = frame.shape
    return call(
        residual_kernel,
        (jax.ShapeDtypeStruct((width // 2, rows), jnp.bfloat16), jax.ShapeDtypeStruct((width // 2, 8), jnp.float32)),
        (core, frame, modulation),
        flops=4 * rows * width,
        moved=3 * rows * width,
        grant=16,
    )


def part_kernel(where_ref, mine_ref, other_ref, heads_ref, start_ref, gate_ref, out_ref, weight):
    group, core = where_ref[1], where_ref[3]
    block = mine_ref.shape[1]
    per_core = mine_ref.shape[0] // 2
    for same, ref in ((True, mine_ref), (False, other_ref)):
        half = group if same else 1 - group
        for index in range(per_core):
            start = pl.multiple_of((index * 2 + half) * block, block)
            weight[pl.ds(start, block), :] = ref[core * per_core + index]
    projected = dot_nn(weight[...], heads_ref[...])
    out_ref[...] = (start_ref[...].astype(jnp.float32) + gate_ref[:, 0:1] * projected).astype(out_ref.dtype)


def add_part(where, mine, other, heads, start, gate, dtype):
    return call(
        part_kernel,
        jax.ShapeDtypeStruct(start.shape, dtype),
        (where, mine, other, heads, start, gate),
        [pltpu.VMEM((start.shape[0], mine.shape[2]), jnp.bfloat16)],
        grant=16,
    )


def swapped(block, axis):
    return lax.ppermute(block, axis, [(0, 1), (1, 0)])


def shifted(block, axis, distance):
    devices = range(lax.axis_size(axis))
    route = [(i - distance, i) for i in devices if i - distance in devices]
    return lax.ppermute(block, axis, route)


def from_partner(block, axis, stride):
    count = lax.axis_size(axis)
    route = []
    for low in range(count):
        high = low | 1 << stride
        if high != low and high < count:
            route += [(low, high), (high, low)]
    return lax.ppermute(block, axis, route)


def attend(queries, kv_all, first_frame, anchor, head_dim):
    frame_count, query_rows, query_width = queries.shape
    key_count = kv_all.shape[1]
    head_count = query_width // head_dim
    block_rows = math.gcd(512, query_rows)
    kv_heads = kv_all.reshape(frame_count + 2, key_count, head_count, 2, head_dim)
    global_idx = first_frame + 0
    use_prev = global_idx > 0
    use_anchor = (anchor != global_idx) & (anchor != global_idx - 1)
    valid_keys = jnp.concatenate(
        [
            jnp.broadcast_to(use_anchor, (key_count,)),
            jnp.broadcast_to(use_prev, (key_count,)),
            jnp.ones((key_count,), bool),
        ]
    )
    frame_queries = queries[0]

    def one_head(head_idx):
        picked = lax.dynamic_index_in_dim(kv_heads, head_idx, 2, keepdims=False)
        key_rows = jnp.concatenate(
            [picked[frame_count + 1, :, 0], picked[frame_count, :, 0], picked[0, :, 0]], 0
        )
        val_rows = jnp.concatenate(
            [picked[frame_count + 1, :, 1], picked[frame_count, :, 1], picked[0, :, 1]], 0
        )
        query_head = lax.dynamic_slice_in_dim(frame_queries, head_idx * head_dim, head_dim, 1)
        query_blocks = query_head.reshape(query_rows // block_rows, block_rows, head_dim)

        def one_block(query_block):
            scores = lax.dot_general(
                query_block, key_rows, (((1,), (1,)), ((), ())), preferred_element_type=jnp.float32
            ) * head_dim ** (-0.5)
            scores = jnp.where(valid_keys[None, :], scores, -1e30)
            row_max = jnp.max(scores, axis=-1, keepdims=True)
            probs = jnp.exp(scores - row_max)
            denominator = jnp.sum(probs, axis=-1, keepdims=True)
            numerator = jnp.dot(
                probs.astype(jnp.bfloat16), val_rows, preferred_element_type=jnp.float32
            )
            return (numerator / denominator).astype(jnp.bfloat16)

        return lax.map(one_block, query_blocks).reshape(query_rows, head_dim)

    per_head = lax.map(one_head, jnp.arange(head_count, dtype=jnp.int32))
    frame_outputs = [jnp.transpose(per_head, (1, 0, 2)).reshape(query_rows, head_count * head_dim)]
    return jnp.stack(frame_outputs)


def by_frames(frames, modulation, w_qkv, w_out, anchor_offsets):
    frame_count, row_count, model_width = frames.shape
    head_local = w_qkv.shape[1]
    head_dim = w_qkv.shape[3]
    my_index = lax.axis_index("frame")
    flat_rows = frames.reshape(frame_count * row_count, model_width).astype(jnp.float32)
    row_mean = jnp.mean(flat_rows, axis=-1, keepdims=True)
    centred = flat_rows - row_mean
    row_var = jnp.mean(centred * centred, axis=-1, keepdims=True)
    normed = centred * lax.rsqrt(row_var + 1e-06)
    hidden = (normed * (1.0 + modulation[1]) + modulation[0]).astype(jnp.bfloat16)
    full_weight = lax.all_gather(w_qkv, "frame", axis=0, tiled=True)
    mixed = jnp.dot(
        hidden,
        full_weight.reshape(model_width, head_local * 3 * head_dim),
        preferred_element_type=jnp.float32,
    )
    mixed = mixed.astype(jnp.bfloat16).reshape(frame_count, row_count, head_local, 3, head_dim)
    queries = mixed[:, :, :, 0, :].reshape(frame_count, row_count, head_local * head_dim)
    keyvals = mixed[:, :, :, 1:, :].reshape(frame_count, row_count, head_local * 2 * head_dim)
    span_count = anchor_offsets.shape[0]
    total_frames = frame_count * lax.axis_size("frame")
    span_len = total_frames // span_count
    first_frame = my_index * frame_count
    mine_span = first_frame // span_len
    anchor = mine_span * span_len + anchor_offsets[mine_span]
    prev_kv = shifted(keyvals[frame_count - 1], "frame", 1)
    holder = anchor // frame_count
    anchor_kv = lax.dynamic_index_in_dim(keyvals, anchor % frame_count, 0, keepdims=False)
    levels = (span_len // frame_count).bit_length() - 1
    for bit_index in range(levels):
        partner = from_partner(anchor_kv, "frame", bit_index)
        take_partner = my_index >> bit_index & 1 != holder >> bit_index & 1
        anchor_kv = jnp.where(take_partner, partner, anchor_kv)
    kv_all = jnp.concatenate([keyvals, prev_kv[None], anchor_kv[None]], 0)
    kv_whole = lax.all_gather(kv_all, "tok", axis=1, tiled=True)
    attended = attend(queries, kv_whole, first_frame, anchor, head_dim)
    flat_attended = attended.reshape(frame_count * row_count, head_local * head_dim)
    term_cols = jnp.dot(
        flat_attended,
        lax.all_gather(w_out, "frame", axis=1, tiled=True),
        preferred_element_type=jnp.float32,
    )
    summed = lax.psum_scatter(term_cols, "head", scatter_dimension=1, tiled=True)
    half_width = summed.shape[1]
    col_start = lax.axis_index("head") * half_width
    residual_in = lax.dynamic_slice_in_dim(flat_rows, col_start, half_width, 1)
    gate_part = lax.dynamic_slice_in_dim(modulation[2], col_start, half_width, 0)
    result = (residual_in + gate_part * summed).astype(jnp.bfloat16)
    return result.reshape(frame_count, row_count, half_width)


def flipped(block, axis, distance):
    return lax.ppermute(block, axis, [(i, i ^ distance) for i in range(lax.axis_size(axis))])


def after(block, other):
    return lax.optimization_barrier((block, other))[0]


def by_heads(frames, modulation, w_qkv, w_out, anchor_offsets):
    _, rows, width = frames.shape
    share, head_local, _, head_dim = w_qkv.shape
    count = lax.axis_size("frame")
    heads = head_local // count
    core = lax.axis_index("head")
    me = lax.axis_index("frame")
    group = lax.axis_index("groups")
    frame = frames[0]
    place = core.reshape(1).astype(jnp.int32)

    tok = lax.axis_index("tok")
    where = jnp.stack([me, group, tok, core]).astype(jnp.int32)

    blocks = jnp.transpose(w_qkv, (1, 2, 3, 0)).reshape(count, heads, 3 * head_dim, share)
    part_rows = -(-3 * head_dim // 32) * 16
    start = tok * (3 * head_dim - part_rows)
    part = lax.dynamic_slice(blocks, (0, group, start, 0), (count, 1, part_rows, share))[:, 0]
    part = jnp.transpose(part, (0, 2, 1))
    part = lax.all_to_all(part, "frame", 0, 0)
    plane = lax.all_to_all(jnp.broadcast_to(part[None], (4, *part.shape)), ("groups", "tok"), 0, 0)
    weight = join_weight(plane, heads, head_dim)
    kv_width = 2 * heads * head_dim

    mine = norm_half(place, frame, modulation)
    arrivals = [mine, flipped(mine, "frame", 1), flipped(mine, "frame", 2)]
    arrivals.append(flipped(arrivals[2], "frame", 1))
    frame_part, gate_part = residual(place, after(frame, arrivals[1]), modulation)

    queries, near, far = [], [], []
    for distance, block in enumerate(arrivals):
        if distance == 3:
            block = after(block, (frame_part, near[0], near[1], near[2]))
        kv, q = project(place, weight, block, swapped(block, "head"), kv_width)
        queries.append(q)
        near.append(kv)
        if distance == 0:
            across = after(swapped(block, "tok"), kv)
            far += project(place, weight, across, swapped(across, "head"), kv_width, False)
        else:
            far.append(swapped(kv, "tok"))
    ids = jnp.stack([me ^ distance for distance in range(count)] + [anchor_offsets[0]]).astype(jnp.int32)
    attended = attend_all(ids, queries, near, far, heads, head_dim)
    arrived = lax.all_to_all(attended, "frame", 0, 0).reshape(count * heads * head_dim, rows)
    arrived_far = swapped(arrived, "head")

    columns = w_out.shape[1] // 2
    w_part = lax.dynamic_slice_in_dim(w_out.T, group * columns, columns, 0)
    w_part = after(w_part, near[-1])
    w_part = lax.all_to_all(jnp.broadcast_to(w_part[None], (count, *w_part.shape)), "frame", 0, 0)
    w_other = swapped(w_part, "groups")
    near_sum = add_part(where, w_part, w_other, arrived, frame_part, gate_part, jnp.float32)
    w_far = [swapped(w, "head") for w in (w_part, w_other)]
    updated = add_part(where, *w_far, arrived_far, near_sum, gate_part, jnp.bfloat16)
    return updated.T[None]


def on_device(frames, modulation, w_qkv, w_out, anchor_offsets):
    count = lax.axis_size("frame")
    fits = (
        frames.shape[0] == 1
        and anchor_offsets.shape[0] == 1
        and count == 4
        and lax.axis_size("groups") == 2
        and lax.axis_size("head") == 2
        and lax.axis_size("tok") == 2
        and w_qkv.shape[1] == 2 * count
        and w_qkv.shape[3] % 8 == 0
        and frames.shape[1] % 256 == 0
        and frames.shape[2] % 32 == 0
    )
    step = by_heads if fits else by_frames
    return step(frames, modulation, w_qkv, w_out, anchor_offsets)


def solution(mesh):
    placed = (
        P(("groups", "frame"), "tok", None),
        P(),
        P("frame", "head", None, None),
        P("head", "frame"),
        P("groups"),
    )
    return jax.shard_map(
        on_device,
        mesh=mesh,
        in_specs=placed,
        out_specs=P(("groups", "frame"), "tok", "head"),
        check_vma=False,
    )
```
